128 devices in a mesh: stream: 32 (over z, y, core), span: 4 (over x).
Axes of the slice: x: 4, y: 4, z: 4, core: 2. Of those that a mesh axis runs over, the one named last changes fastest.
Arguments:
- populations: float32 [19, 1024, 8192], P(None, 'stream', 'span'), as said below
- camera: int32 [32], P('stream'), may hold values from 0 to 1
- active_list: int32 [32, 4, 32], P('stream', 'span'), may hold values from 0 to 32, as said below
- tile_order: int32 [32, 8], P('stream'), may hold values from 0 to 7, each once within a row
Outputs:
- final_populations: float32 [19, 1024, 8192], P(None, 'stream', 'span')
- tile_image: float32 [256, 4, 256], P(('stream', 'span'))
The draws below stay inside these ranges and needn't reach their ends.
Inputs may be any that keep to these rules, and one draw needn't show every extreme that they name: `active_list`: each row lists the distinct numbers of the active bricks of one device in rising order and then the value 32 in the remaining places; the share of active bricks differs widely between devices, and some device lists all 32 of its bricks. `populations`: populations are positive.
All inputs are finite; a program needn't handle non-finite values.
Results may differ from the reference program's by a relative error of at most 0.0001.
Values sent between devices are 32-bit elements; how exact they have to be, the bound alone decides.
A program may use at most 128 MiB of HBM per device.

```python
import math
import jax
import jax.numpy as jnp
from jax import lax

CX = 32
CY = 32
NZ = 64
STEPS = 3
BX = 4
BY = 8
NX = 1024
NY = 128
SLABS = 32
SPANS = 4
BRICKS_DEV = 32
TILES_SLAB = 8
TILES = 256


VELOCITIES = ((0, 0, 0), (1, 0, 0), (-1, 0, 0), (0, 1, 0), (0, -1, 0), (0, 0, 1), (0, 0, -1), (1, 1, 0), (-1, -1, 0), (1, -1, 0), (-1, 1, 0), (1, 0, 1), (-1, 0, -1), (1, 0, -1), (-1, 0, 1), (0, 1, 1), (0, -1, -1), (0, 1, -1), (0, -1, 1))


WEIGHTS = (1.0 / 3.0,) + (1.0 / 18.0,) * 6 + (1.0 / 36.0,) * 12


def draw_populations(key, part):
    key = jax.random.fold_in(key, 3)
    subkeys = jax.random.split(key, 3)
    extent = (NX, NY * NZ)
    density = jax.random.uniform(subkeys[0], extent, jnp.float32, 0.8, 1.2)
    velocity = 0.08 * jax.random.truncated_normal(subkeys[1], -2.5, 2.5, (3,) + extent, jnp.float32)
    jitter = jax.random.uniform(subkeys[2], (19,) + extent, jnp.float32, -0.3, 0.3)
    square = velocity[0] * velocity[0] + velocity[1] * velocity[1] + velocity[2] * velocity[2]
    layers = []
    for index in range(19):
        projected = jnp.zeros_like(density)
        for dimension in range(3):
            component = VELOCITIES[index][dimension]
            if component != 0:
                projected = projected + component * velocity[dimension]
        balance = WEIGHTS[index] * density * (1.0 + 3.0 * projected + 4.5 * projected * projected - 1.5 * square)
        layers.append(balance * (1.0 + jitter[index]))
    return jnp.stack(layers).astype(jnp.float32)


def draw_active_list(key, part):
    key = jax.random.fold_in(key, 7)
    subkeys = jax.random.split(key, 3)
    level = jax.random.randint(subkeys[0], (SLABS, SPANS, 1), 0, 16)
    chance = level * level + 8
    score = jax.random.randint(subkeys[1], (SLABS, SPANS, BRICKS_DEV), 0, 256)
    chosen = jax.random.randint(subkeys[2], (), 0, SLABS * SPANS)
    device = lax.broadcasted_iota(jnp.int32, (SLABS, SPANS, 1), 0) * SPANS + lax.broadcasted_iota(jnp.int32, (SLABS, SPANS, 1), 1)
    keeping = (score < chance) | (device == chosen)
    number = lax.broadcasted_iota(jnp.int32, (SLABS, SPANS, BRICKS_DEV), 2)
    ranking = jnp.where(keeping, number, number + BRICKS_DEV)
    ordered = jnp.sort(ranking, axis=2)
    return jnp.where(ordered < BRICKS_DEV, ordered, BRICKS_DEV).astype(jnp.int32)


def place_ends(values, rng, low, largest):
    dims = values.shape
    place = [jax.random.randint(jax.random.fold_in(rng, axis), (), 0, dims[axis]) for axis in range(len(dims))]
    values = values.at[tuple(place)].set(low)
    longest = dims.index(max(dims))
    place[longest] = (place[longest] + 1) % dims[longest]
    return values.at[tuple(place)].set(largest)


def setup_inputs(seed: int = 0) -> dict:
    arg_keys = jax.random.split(jax.random.key(seed), 5)
    populations = draw_populations(jax.random.fold_in(arg_keys[4], 71), 0)
    camera = place_ends(jax.random.randint(arg_keys[1], (SLABS,), 0, 2), jax.random.fold_in(arg_keys[1], 1), 0, 1).astype(jnp.int32)
    active_list = draw_active_list(jax.random.fold_in(arg_keys[4], 71), 0)
    tile_order = jax.vmap(lambda own: jax.random.permutation(own, TILES_SLAB))(jax.random.split(arg_keys[3], SLABS)).reshape((SLABS, TILES_SLAB)).astype(jnp.int32)
    return {"populations": populations, "camera": camera, "active_list": active_list, "tile_order": tile_order}


VELOCITIES = ((0, 0, 0), (1, 0, 0), (-1, 0, 0), (0, 1, 0), (0, -1, 0), (0, 0, 1), (0, 0, -1), (1, 1, 0), (-1, -1, 0), (1, -1, 0), (-1, 1, 0), (1, 0, 1), (-1, 0, -1), (1, 0, -1), (-1, 0, 1), (0, 1, 1), (0, -1, -1), (0, 1, -1), (0, -1, 1))
OPPOSITE = (0, 2, 1, 4, 3, 6, 5, 8, 7, 10, 9, 12, 11, 14, 13, 16, 15, 18, 17)
WEIGHTS = (1.0 / 3.0,) + (1.0 / 18.0,) * 6 + (1.0 / 36.0,) * 12
STRESS_PAIRS = ((0, 0, 1.0), (1, 1, 1.0), (2, 2, 1.0), (0, 1, 2.0), (0, 2, 2.0), (1, 2, 2.0))
TAU_ZERO = 0.55
SMAGORINSKY = 0.17
VORTEX_SCALE = 0.003
SPEED_SCALE = 0.08
OPACITY_GAIN = 0.03

def directional(fractions, dimension):
    total = jnp.zeros_like(fractions[0])
    for index in range(19):
        component = VELOCITIES[index][dimension]
        if component > 0:
            total = total + fractions[index]
        elif component < 0:
            total = total - fractions[index]
    return total

def collide(fractions):
    density = lax.optimization_barrier(jnp.sum(fractions, axis=0))
    inverse = 1.0 / density
    velocity = [directional(fractions, dimension) * inverse for dimension in range(3)]
    square = velocity[0] * velocity[0] + velocity[1] * velocity[1] + velocity[2] * velocity[2]
    departure = []
    for index in range(19):
        projected = jnp.zeros_like(density)
        for dimension in range(3):
            component = VELOCITIES[index][dimension]
            if component != 0:
                projected = projected + component * velocity[dimension]
        balance = WEIGHTS[index] * density * (1.0 + 3.0 * projected + 4.5 * projected * projected - 1.5 * square)
        departure.append(fractions[index] - balance)
    magnitude = jnp.zeros_like(density)
    for first, second, factor in STRESS_PAIRS:
        moment = jnp.zeros_like(density)
        for index in range(19):
            product = VELOCITIES[index][first] * VELOCITIES[index][second]
            if product > 0:
                moment = moment + departure[index]
            elif product < 0:
                moment = moment - departure[index]
        magnitude = magnitude + factor * moment * moment
    magnitude = jnp.sqrt(magnitude)
    relaxation = 0.5 * (TAU_ZERO + jnp.sqrt(TAU_ZERO * TAU_ZERO + 18.0 * math.sqrt(2.0) * SMAGORINSKY * SMAGORINSKY * magnitude * inverse))
    return jnp.stack([fractions[index] - departure[index] / relaxation for index in range(19)])

def stream_full(post):
    level = lax.broadcasted_iota(jnp.int32, post.shape[1:], 2)
    moved = []
    for index in range(19):
        along_x, along_y, along_z = VELOCITIES[index]
        shifted = jnp.roll(post[index], (along_x, along_y, along_z), axis=(0, 1, 2))
        if along_z != 0:
            wall = 0 if along_z > 0 else NZ - 1
            shifted = jnp.where(level == wall, post[OPPOSITE[index]], shifted)
        moved.append(shifted)
    return jnp.stack(moved)

def invariant_full(velocity):
    grad_x = (jnp.roll(velocity, -1, axis=1) - jnp.roll(velocity, 1, axis=1)) * 0.5
    grad_y = (jnp.roll(velocity, -1, axis=2) - jnp.roll(velocity, 1, axis=2)) * 0.5
    padded = jnp.concatenate([-velocity[:, :, :, :1], velocity, -velocity[:, :, :, -1:]], axis=3)
    grad_z = (padded[:, :, :, 2:] - padded[:, :, :, :-2]) * 0.5
    grads = (grad_x, grad_y, grad_z)
    total = jnp.zeros_like(velocity[0])
    for first in range(3):
        for second in range(3):
            total = total + grads[second][first] * grads[first][second]
    return -0.5 * total

def reference(populations, camera, active_list, tile_order):
    current = populations.reshape(19, NX, NY, NZ)
    for section in range(STEPS):
        current = stream_full(collide(current))
    final_populations = current.reshape(19, NX, NY * NZ)
    density = lax.optimization_barrier(jnp.sum(current, axis=0))
    inverse = 1.0 / density
    velocity = jnp.stack([directional(current, dimension) * inverse for dimension in range(3)])
    vortex = invariant_full(velocity)
    number = lax.broadcasted_iota(jnp.int32, (BRICKS_DEV, BRICKS_DEV), 0)
    present = jnp.any(active_list[:, :, None, :] == number[None, None, :, :], axis=3)
    present = present.astype(jnp.float32).reshape(SLABS, SPANS, CX // BX, CY // BY)
    present = present.transpose(0, 2, 1, 3)
    present = jnp.broadcast_to(present[:, :, None, :, :, None], (SLABS, CX // BX, BX, SPANS, CY // BY, BY))
    cell_mask = present.reshape(NX, NY)[:, :, None]
    flipped = jnp.repeat(camera == 1, CX)[:, None, None]

    def oriented(field):
        return jnp.where(flipped, jnp.flip(field, 1), field)
    opacity = oriented((1.0 - jnp.exp(-OPACITY_GAIN * jax.nn.softplus(vortex / VORTEX_SCALE))) * cell_mask)
    colours = [oriented(jax.nn.sigmoid(vortex / VORTEX_SCALE)), oriented(jax.nn.sigmoid(velocity[0] / SPEED_SCALE)), oriented(jax.nn.sigmoid(velocity[2] / SPEED_SCALE))]
    through = jnp.cumprod(1.0 - opacity, axis=1)
    before = jnp.concatenate([jnp.ones_like(through[:, :1]), through[:, :-1]], axis=1)
    weight = opacity * before
    shades = [lax.optimization_barrier(jnp.sum(colour * weight, axis=1)) for colour in colours]
    shades.append(through[:, -1])
    tiles = jnp.stack(shades).reshape(4, TILES, BX * NZ).transpose(1, 0, 2)
    places = (jnp.arange(SLABS, dtype=jnp.int32)[:, None] * TILES_SLAB + tile_order).reshape(-1)
    tile_image = jnp.take(tiles, places, axis=0)
    return (final_populations, tile_image)
```

```python
import functools
import math

import jax
import jax.numpy as jnp
from jax import lax
from jax.experimental import pallas as pl
from jax.experimental.pallas import tpu as pltpu
from jax.sharding import PartitionSpec as P

MESH = pl.DeviceIdType.MESH

NZ = 64
LANES = 128
POPS = 19
PLANES = 32
COLUMNS = 16
TOP = 8
ROWS = 48
BLOCKS = PLANES // 8

VELOCITIES = (
    (0, 0, 0),
    (1, 0, 0),
    (-1, 0, 0),
    (0, 1, 0),
    (0, -1, 0),
    (0, 0, 1),
    (0, 0, -1),
    (1, 1, 0),
    (-1, -1, 0),
    (1, -1, 0),
    (-1, 1, 0),
    (1, 0, 1),
    (-1, 0, -1),
    (1, 0, -1),
    (-1, 0, 1),
    (0, 1, 1),
    (0, -1, -1),
    (0, 1, -1),
    (0, -1, 1),
)
OPPOSITE = (0, 2, 1, 4, 3, 6, 5, 8, 7, 10, 9, 12, 11, 14, 13, 16, 15, 18, 17)
TAU_ZERO = 0.55
SMAGORINSKY = 0.17
VORTEX_SCALE = 0.003
SPEED_SCALE = 0.08
OPACITY_GAIN = 0.03

ORDER = (0, 5, 6, 9, 1, 11, 13, 7, 3, 15, 17, 10, 2, 12, 14, 8, 4, 16, 18)
SLOT = tuple(ORDER.index(index) for index in range(POPS))
X_UP = (3, 5)
X_DOWN = (11, 5)
Y_UP = (7, 5)
Y_DOWN = (15, 4)

PLACES = COLUMNS + 2
SECTIONS = ((0, 1), (1, 3), (3, 5), (5, 7), (7, 8))
X_MESSAGES = 2 * len(SECTIONS)
POST_MESSAGES = X_MESSAGES + 7
SPEED_MESSAGES = X_MESSAGES + 2
POST_PHASES = 3
SPEED_BASE = POST_PHASES * POST_MESSAGES
TILE_BASE = SPEED_BASE + SPEED_MESSAGES
MESSAGES = TILE_BASE + 3


def reciprocal(value):
    guess = pl.reciprocal(value, approx=True)
    return guess * (2.0 - value * guess)


def moments(f):
    pair = {index: f[index] + f[index + 1] for index in range(1, POPS, 2)}
    gap = {index: f[index] - f[index + 1] for index in range(1, POPS, 2)}
    flow = (
        (gap[1] + gap[7]) + (gap[9] + gap[11]) + gap[13],
        (gap[3] + gap[7]) + (gap[15] - gap[9]) + gap[17],
        (gap[5] + gap[11]) + (gap[15] - gap[13]) - gap[17],
    )
    around_xy = pair[7] + pair[9]
    around_xz = pair[11] + pair[13]
    around_yz = pair[15] + pair[17]
    along_x = pair[1] + (around_xy + around_xz)
    density = (f[0] + pair[3]) + (pair[5] + around_yz) + along_x
    return pair, flow, (around_xy, around_xz, around_yz), along_x, density


def collide(f):
    pair, flow, around, along_x, density = moments(f)
    along_y = pair[3] + (around[0] + around[2])
    along_z = pair[5] + (around[1] + around[2])
    inverse = reciprocal(density)
    triple = 3.0 * inverse
    ninth = 9.0 * inverse
    vx, vy, vz = [part * triple for part in flow]
    vxx, vyy, vzz = vx * vx, vy * vy, vz * vz
    vxy, vxz, vyz = vx * vy, vx * vz, vy * vz
    qxx = ninth * along_x - (3.0 + vxx)
    qyy = ninth * along_y - (3.0 + vyy)
    qzz = ninth * along_z - (3.0 + vzz)
    qxy = ninth * (pair[7] - pair[9]) - vxy
    qxz = ninth * (pair[11] - pair[13]) - vxz
    qyz = ninth * (pair[15] - pair[17]) - vyz
    cross = qxy * qxy + qxz * qxz + qyz * qyz
    square = (qxx * qxx + qyy * qyy) + (qzz * qzz + (cross + cross))
    magnitude = square * lax.rsqrt(jnp.maximum(square, 1e-30))
    inner = TAU_ZERO * TAU_ZERO + (18.0 * math.sqrt(2.0) * SMAGORINSKY * SMAGORINSKY / 9.0) * magnitude
    rate = 2.0 * reciprocal(TAU_ZERO + inner * lax.rsqrt(inner))
    keep = 1.0 - rate
    weight = (rate * density) * (1.0 / 36.0)
    bx, by, bz = weight * vx, weight * vy, weight * vz
    axx, ayy, azz = weight * vxx, weight * vyy, weight * vzz
    hx, hy, hz = 0.5 * axx, 0.5 * ayy, 0.5 * azz
    base = weight - (hx + hy + hz) * (1.0 / 3.0)
    double = base + base
    out = [None] * POPS
    out[0] = keep * f[0] + 12.0 * base
    for index, even, odd in ((1, double + axx, bx + bx), (3, double + ayy, by + by), (5, double + azz, bz + bz)):
        out[index] = keep * f[index] + (even + odd)
        out[index + 1] = keep * f[index + 1] + (even - odd)
    for index, first, second, half_first, half_second, mixed in (
        (7, bx, by, hx, hy, weight * vxy),
        (11, bx, bz, hx, hz, weight * vxz),
        (15, by, bz, hy, hz, weight * vyz),
    ):
        middle = base + (half_first + half_second)
        same, other = middle + mixed, middle - mixed
        plus, minus = first + second, first - second
        out[index] = keep * f[index] + (same + plus)
        out[index + 1] = keep * f[index + 1] + (same - plus)
        out[index + 2] = keep * f[index + 2] + (other + minus)
        out[index + 3] = keep * f[index + 3] + (other - minus)
    return out


def kernel(
    spans,
    streams,
    populations,
    camera,
    active_list,
    tile_order,
    final,
    tile_image,
    field,
    post0,
    post1,
    post2,
    speed,
    foot,
    outgoing,
    incoming,
    send_sem,
    recv_sem,
    load_sem,
    store_sem,
    own_sem,
):
    stream = lax.axis_index("stream")
    span = lax.axis_index("span")
    stream_up = lax.rem(stream + 1, streams)
    stream_down = lax.rem(stream + streams - 1, streams)
    span_up = lax.rem(span + 1, spans)
    span_down = lax.rem(span + spans - 1, spans)
    span_far = lax.rem(span + 2, spans)

    loads = []
    for k in range(COLUMNS // 2):
        for side in range(2):
            column = k if side == 0 else COLUMNS - 1 - k
            loads.append(
                pltpu.make_async_copy(
                    populations.at[:, :, pl.ds(column * LANES, LANES)],
                    field.at[:, 2 * k + side],
                    load_sem.at[2 * k + side],
                )
            )
            loads[-1].start()

    barrier = pltpu.get_barrier_semaphore()
    partners = (
        (stream_up, span),
        (stream_down, span),
        (stream, span_up),
        (stream, span_down),
        (stream_up, span_up),
        (stream_up, span_down),
        (stream_down, span_up),
        (stream_down, span_down),
        (stream, span_far),
    )
    for partner in partners:
        pl.semaphore_signal(barrier, inc=1, device_id=partner, device_id_type=MESH)

    lane = lax.broadcasted_iota(jnp.int32, (8, LANES), 1)
    upper = lane >= NZ
    level = lax.rem(lane, NZ)
    floor = level == 0
    ceiling = level == NZ - 1

    def remote(source, target, number, device):
        return pltpu.make_async_remote_copy(
            src_ref=source,
            dst_ref=target,
            send_sem=send_sem.at[number],
            recv_sem=recv_sem.at[number],
            device_id=device,
            device_id_type=MESH,
        )

    def x_copies(buffer, base, section, up, down):
        first, last = SECTIONS[section]
        places = pl.ds(2 * first + 2, 2 * (last - first))
        return [
            remote(
                buffer.at[pl.ds(*up), places, pl.ds(TOP + PLANES - 1, 1)],
                buffer.at[pl.ds(*up), places, pl.ds(TOP - 1, 1)],
                base + 2 * section,
                (stream_up, span),
            ),
            remote(
                buffer.at[pl.ds(*down), places, pl.ds(TOP, 1)],
                buffer.at[pl.ds(*down), places, pl.ds(TOP + PLANES, 1)],
                base + 2 * section + 1,
                (stream_down, span),
            ),
        ]

    def y_copy(buffer, slots, number, upwards):
        rows = pl.ds(TOP, PLANES)
        if upwards:
            return remote(
                buffer.at[pl.ds(*slots), 3, rows], buffer.at[pl.ds(*slots), 0, rows], number, (stream, span_up)
            )
        return remote(
            buffer.at[pl.ds(*slots), 2, rows], buffer.at[pl.ds(*slots), 1, rows], number, (stream, span_down)
        )

    def post_edges(buffer, base):
        number = base + X_MESSAGES
        low, high = TOP, TOP + PLANES - 1
        copies = [
            y_copy(buffer, Y_UP, number, True),
            y_copy(buffer, Y_DOWN, number + 1, False),
            y_copy(buffer, (SLOT[9], 1), number + 2, False),
        ]
        for place, (index, source, target, device) in enumerate(
            (
                (7, (3, high), (0, TOP - 1), (stream_up, span_up)),
                (10, (3, low), (0, TOP + PLANES), (stream_down, span_up)),
                (8, (2, low), (1, TOP + PLANES), (stream_down, span_down)),
                (9, (2, high), (1, TOP - 1), (stream_up, span_down)),
            )
        ):
            copies.append(
                remote(
                    buffer.at[SLOT[index], source[0], pl.ds(source[1], 1)],
                    buffer.at[SLOT[index], target[0], pl.ds(target[1], 1)],
                    number + 3 + place,
                    device,
                )
            )
        return copies

    def streamed(buffer, place, before, after, block):
        top = TOP + 8 * block
        values = []
        for index in range(POPS):
            along_x, along_y, along_z = VELOCITIES[index]
            rows = pl.ds(top - along_x, 8)
            value = buffer[SLOT[index], place, rows]
            if along_y == 1:
                value = jnp.where(upper, buffer[SLOT[index], before, rows], value)
            elif along_y == -1:
                value = jnp.where(upper, value, buffer[SLOT[index], after, rows])
            shift = ((NZ if along_y else 0) + along_z) % LANES
            if shift:
                value = pltpu.roll(value, shift, 1)
            if along_z:
                value = jnp.where(
                    floor if along_z > 0 else ceiling,
                    buffer[SLOT[OPPOSITE[index]], place, pl.ds(top, 8)],
                    value,
                )
            values.append(value)
        return values

    def neighbours(k, side):
        if side == 0:
            after = 17 if isinstance(k, int) and k == 7 else 2 * k + 4
            return 2 * k + 2, 2 * k, after
        before = 16 if isinstance(k, int) and k == 7 else 2 * k + 5
        return 2 * k + 3, before, 2 * k + 1

    def columns(section, work):
        first, last = SECTIONS[section]
        if last - first == 1:
            for side in range(2):
                work(first, side)
        else:

            def body(k, carry):
                for side in range(2):
                    work(k, side)
                return carry

            lax.fori_loop(first, last, body, 0)

    sent = []

    def send(copies):
        for copy in copies:
            copy.start()
        sent.extend(copies)

    def first_work(k, side):
        place = 2 * k + side
        for block in range(BLOCKS):
            rows = pl.ds(8 * block, 8)
            out = collide([field[index, place, rows] for index in range(POPS)])
            for index in range(POPS):
                post0[SLOT[index], place + 2, pl.ds(TOP + 8 * block, 8)] = out[index]

    buffers = (post0, post1, post2)
    edges = [post_edges(buffer, number * POST_MESSAGES) for number, buffer in enumerate(buffers)]
    sides = [
        [x_copies(buffer, number * POST_MESSAGES, section, X_UP, X_DOWN) for section in range(len(SECTIONS))]
        for number, buffer in enumerate(buffers)
    ]
    for section, (first, last) in enumerate(SECTIONS):
        for number in range(2 * first, 2 * last):
            loads[number].wait()
        columns(section, first_work)
        if section == 0:
            pl.semaphore_wait(barrier, len(partners))
            send(edges[0])
        send(sides[0][section])

    def await_rims(edge, side, section):
        if section == 0:
            for copy in edge:
                copy.wait_recv()
            for copy in side[0]:
                copy.wait_recv()
        if section + 1 < len(SECTIONS):
            for copy in side[section + 1]:
                copy.wait_recv()

    for phase in (1, 2):
        source, target = buffers[phase - 1], buffers[phase]

        def step_work(k, side):
            place, before, after = neighbours(k, side)
            for block in range(BLOCKS):
                out = collide(streamed(source, place, before, after, block))
                for index in range(POPS):
                    target[SLOT[index], place, pl.ds(TOP + 8 * block, 8)] = out[index]

        for section in range(len(SECTIONS)):
            await_rims(edges[phase - 1], sides[phase - 1], section)
            columns(section, step_work)
            if section == 0:
                send(edges[phase])
            send(sides[phase][section])

    def last_work(k, side):
        place, before, after = neighbours(k, side)
        for block in range(BLOCKS):
            values = streamed(post2, place, before, after, block)
            for index in range(POPS):
                field[index, place - 2, pl.ds(8 * block, 8)] = values[index]
            _, flow, _, _, density = moments(values)
            inverse = reciprocal(density)
            for dimension in range(3):
                speed[dimension, place, pl.ds(TOP + 8 * block, 8)] = flow[dimension] * inverse

    speed_edges = [
        y_copy(speed, (0, 3), SPEED_BASE + X_MESSAGES, True),
        y_copy(speed, (0, 3), SPEED_BASE + X_MESSAGES + 1, False),
    ]
    speed_sides = [x_copies(speed, SPEED_BASE, section, (0, 3), (0, 3)) for section in range(len(SECTIONS))]
    stores = []
    for section, (first, last) in enumerate(SECTIONS):
        await_rims(edges[2], sides[2], section)
        columns(section, last_work)
        if section == 0:
            send(speed_edges)
        send(speed_sides[section])
        for k in range(first, last):
            for side in range(2):
                column = k if side == 0 else COLUMNS - 1 - k
                stores.append(
                    pltpu.make_async_copy(
                        field.at[:, 2 * k + side],
                        final.at[:, :, pl.ds(column * LANES, LANES)],
                        store_sem.at[2 * k + side],
                    )
                )
                stores[-1].start()

    bits = jnp.int32(0)
    for entry in range(32):
        number = active_list[0, 0, entry]
        bits = bits | jnp.where(number < 32, jnp.left_shift(jnp.int32(1), jnp.minimum(number, 31)), 0)
    falling = jnp.full((8, LANES), camera[0], jnp.int32) == 1
    leading = falling == upper
    bits = jnp.full((8, LANES), bits, jnp.int32)
    corner = 4 * (lax.broadcasted_iota(jnp.int32, (8, LANES), 0) // 4)

    def ray(k, side, block, sums):
        place, before, after = neighbours(k, side)
        column = k if side == 0 else COLUMNS - 1 - k
        top = TOP + 8 * block
        rows = pl.ds(top, 8)
        centre = [speed[dimension, place, rows] for dimension in range(3)]
        slope_x, slope_y, slope_z = [], [], []
        for dimension in range(3):
            here = centre[dimension]
            slope_x.append(speed[dimension, place, pl.ds(top + 1, 8)] - speed[dimension, place, pl.ds(top - 1, 8)])
            behind = here - speed[dimension, before, rows]
            ahead = speed[dimension, after, rows] - here
            slope_y.append(pltpu.roll(jnp.where(upper, behind, ahead), NZ, 1))
            above = jnp.where(ceiling, -here, pltpu.roll(here, LANES - 1, 1))
            below = jnp.where(floor, -here, pltpu.roll(here, 1, 1))
            slope_z.append(above - below)
        cross = slope_x[1] * slope_y[0] + slope_x[2] * slope_z[0] + slope_y[2] * slope_z[1]
        total = slope_x[0] * slope_x[0] + slope_y[1] * slope_y[1] + slope_z[2] * slope_z[2] + (cross + cross)
        vortex = total * (-0.125 / VORTEX_SCALE)
        small = jnp.exp(-jnp.abs(vortex))
        one = 1.0 + small
        share = reciprocal(one)
        colours = [jnp.where(vortex >= 0.0, share, small * share)]
        for dimension in (0, 2):
            colours.append(reciprocal(1.0 + jnp.exp(centre[dimension] * (-1.0 / SPEED_SCALE))))
        passing = jnp.exp(-OPACITY_GAIN * (jnp.maximum(vortex, 0.0) + jnp.log(one)))
        brick = corner + (8 * block + column // 4)
        passing = jnp.where((jnp.right_shift(bits, brick) & 1) == 1, passing, 1.0)
        opacity = 1.0 - passing
        other = pltpu.roll(passing, NZ, 1)
        both = passing * other
        weight = opacity * jnp.where(leading, 1.0, other)
        from_back = falling if side == 0 else jnp.logical_not(falling)
        through = sums[3]
        weight = weight * jnp.where(from_back, 1.0, through)
        fade = jnp.where(from_back, both, 1.0)
        return tuple(sums[n] * fade + colours[n] * weight for n in range(3)) + (through * both,)

    start = tuple(jnp.zeros((8, LANES), jnp.float32) for _ in range(3)) + (jnp.ones((8, LANES), jnp.float32),)
    sums = tuple(start for _ in range(2 * BLOCKS))
    for section, (first, last) in enumerate(SECTIONS):
        await_rims(speed_edges, speed_sides, section)

        def rays(k, sums):
            return tuple(
                ray(k, side, block, sums[side * BLOCKS + block]) for side in range(2) for block in range(BLOCKS)
            )

        if last - first == 1:
            sums = rays(first, sums)
        else:
            sums = lax.fori_loop(first, last, rays, sums)

    for block in range(BLOCKS):
        low, high = sums[block], sums[BLOCKS + block]
        front = [jnp.where(falling, b, a) for a, b in zip(low, high)]
        back = [jnp.where(falling, a, b) for a, b in zip(low, high)]
        for number in range(4):
            if number < 3:
                half = front[number] + front[3] * back[number]
                value = half + pltpu.roll(half, NZ, 1)
            else:
                value = front[3] * back[3]
            for part in range(2):
                foot[2 * block + part, pl.ds(4 * number, 4)] = value[4 * part : 4 * part + 4]

    for number in range(8):
        outgoing[number] = foot[tile_order[0, number]]
    tiles = []
    for hop, target in enumerate((span_up, span_down, span_far)):
        tiles.append(
            remote(
                outgoing.at[pl.ds(2 * target, 2)], incoming.at[span], TILE_BASE + hop, (stream, target)
            )
        )
    send(tiles)
    own = pltpu.make_async_copy(outgoing.at[pl.ds(2 * span, 2)], incoming.at[span], own_sem)
    own.start()
    own.wait()
    for copy in tiles:
        copy.wait_recv()
    wide = jnp.broadcast_to(camera[0], (16, LANES)) == 1
    upper_row = lax.broadcasted_iota(jnp.int32, (1, LANES), 1) >= NZ
    for tile in range(2):
        sheets = [incoming[source, tile] for source in range(spans)]
        colour = sheets[0][:12]
        through = sheets[0][12:]
        for source in range(1, spans):
            sheet = sheets[source]
            fade = jnp.concatenate([sheet[12:]] * 3, axis=0)
            veil = jnp.concatenate([through] * 3, axis=0)
            colour = jnp.where(wide[:12], colour * fade + sheet[:12], colour + veil * sheet[:12])
            through = through * sheet[12:]
        for number in range(4):
            quad = colour[4 * number : 4 * number + 4] if number < 3 else through
            for part in range(2):
                tile_image[tile, pl.ds(number, 1), pl.ds(part * LANES, LANES)] = jnp.where(
                    upper_row, quad[2 * part + 1 : 2 * part + 2], quad[2 * part : 2 * part + 1]
                )

    for copy in sent:
        copy.wait_send()
    for copy in stores:
        copy.wait()


def on_device(populations, camera, active_list, tile_order):
    spans = lax.axis_size("span")
    streams = lax.axis_size("stream")
    vmem = functools.partial(pl.BlockSpec, memory_space=pltpu.VMEM)
    smem = functools.partial(pl.BlockSpec, memory_space=pltpu.SMEM)
    anywhere = functools.partial(pl.BlockSpec, memory_space=pl.ANY)
    post = pltpu.VMEM((POPS, PLACES, ROWS, LANES), jnp.float32)
    return pl.pallas_call(
        functools.partial(kernel, spans, streams),
        out_shape=(
            jax.ShapeDtypeStruct(populations.shape, jnp.float32),
            jax.ShapeDtypeStruct((2, 4, 256), jnp.float32),
        ),
        in_specs=[anywhere(), smem(), smem(), smem()],
        out_specs=(anywhere(), vmem()),
        scratch_shapes=[
            pltpu.VMEM((POPS, COLUMNS, PLANES, LANES), jnp.float32),
            post,
            post,
            post,
            pltpu.VMEM((3, PLACES, ROWS, LANES), jnp.float32),
            pltpu.VMEM((8, 16, LANES), jnp.float32),
            pltpu.VMEM((8, 16, LANES), jnp.float32),
            pltpu.VMEM((spans, 2, 16, LANES), jnp.float32),
            pltpu.SemaphoreType.DMA((MESSAGES,)),
            pltpu.SemaphoreType.DMA((MESSAGES,)),
            pltpu.SemaphoreType.DMA((COLUMNS,)),
            pltpu.SemaphoreType.DMA((COLUMNS,)),
            pltpu.SemaphoreType.DMA,
        ],
        compiler_params=pltpu.CompilerParams(
            collective_id=0, has_side_effects=True, vmem_limit_bytes=48 * 1024 * 1024
        ),
    )(populations, camera, active_list, tile_order)


def solution(mesh):
    placed = (P(None, "stream", "span"), P("stream"), P("stream", "span", None), P("stream", None))
    return jax.shard_map(
        on_device,
        mesh=mesh,
        in_specs=placed,
        out_specs=(P(None, "stream", "span"), P(("stream", "span"), None, None)),
        check_vma=False,
    )
```

```python
import functools
import math

import jax
import jax.numpy as jnp
from jax import lax
from jax.experimental import pallas as pl
from jax.experimental.pallas import tpu as pltpu
from jax.sharding import PartitionSpec as P

MESH = pl.DeviceIdType.MESH

NZ = 64
LANES = 128
POPS = 19
PLANES = 32
COLUMNS = 16
TOP = 8
ROWS = 48
BLOCKS = PLANES // 8

VELOCITIES = (
    (0, 0, 0),
    (1, 0, 0),
    (-1, 0, 0),
    (0, 1, 0),
    (0, -1, 0),
    (0, 0, 1),
    (0, 0, -1),
    (1, 1, 0),
    (-1, -1, 0),
    (1, -1, 0),
    (-1, 1, 0),
    (1, 0, 1),
    (-1, 0, -1),
    (1, 0, -1),
    (-1, 0, 1),
    (0, 1, 1),
    (0, -1, -1),
    (0, 1, -1),
    (0, -1, 1),
)
OPPOSITE = (0, 2, 1, 4, 3, 6, 5, 8, 7, 10, 9, 12, 11, 14, 13, 16, 15, 18, 17)
TAU_ZERO = 0.55
SMAGORINSKY = 0.17
VORTEX_SCALE = 0.003
SPEED_SCALE = 0.08
OPACITY_GAIN = 0.03

ORDER = (0, 5, 6, 9, 1, 11, 13, 7, 3, 15, 17, 10, 2, 12, 14, 8, 4, 16, 18)
SLOT = tuple(ORDER.index(index) for index in range(POPS))
X_UP = (3, 5)
X_DOWN = (11, 5)
Y_PACKS = (((7, 3), (15, 17), (10, None)), ((8, 4), (16, 18), (9, None)))

PLACES = COLUMNS + 2
POST_MESSAGES = 8
SPEED_BASE = 3 * POST_MESSAGES
TILE_BASE = SPEED_BASE + 4
MESSAGES = TILE_BASE + 3


def reciprocal(value):
    guess = pl.reciprocal(value, approx=True)
    return guess * (2.0 - value * guess)


def moments(f):
    pair = {index: f[index] + f[index + 1] for index in range(1, POPS, 2)}
    gap = {index: f[index] - f[index + 1] for index in range(1, POPS, 2)}
    flow = (
        (gap[1] + gap[7]) + (gap[9] + gap[11]) + gap[13],
        (gap[3] + gap[7]) + (gap[15] - gap[9]) + gap[17],
        (gap[5] + gap[11]) + (gap[15] - gap[13]) - gap[17],
    )
    around_xy = pair[7] + pair[9]
    around_xz = pair[11] + pair[13]
    around_yz = pair[15] + pair[17]
    along_x = pair[1] + (around_xy + around_xz)
    density = (f[0] + pair[3]) + (pair[5] + around_yz) + along_x
    return pair, flow, (around_xy, around_xz, around_yz), along_x, density


def collide(f):
    pair, flow, around, along_x, density = moments(f)
    along_y = pair[3] + (around[0] + around[2])
    along_z = pair[5] + (around[1] + around[2])
    inverse = reciprocal(density)
    triple = 3.0 * inverse
    ninth = 9.0 * inverse
    vx, vy, vz = [part * triple for part in flow]
    vxx, vyy, vzz = vx * vx, vy * vy, vz * vz
    vxy, vxz, vyz = vx * vy, vx * vz, vy * vz
    qxx = ninth * along_x - (3.0 + vxx)
    qyy = ninth * along_y - (3.0 + vyy)
    qzz = ninth * along_z - (3.0 + vzz)
    qxy = ninth * (pair[7] - pair[9]) - vxy
    qxz = ninth * (pair[11] - pair[13]) - vxz
    qyz = ninth * (pair[15] - pair[17]) - vyz
    cross = qxy * qxy + qxz * qxz + qyz * qyz
    square = (qxx * qxx + qyy * qyy) + (qzz * qzz + (cross + cross))
    magnitude = square * lax.rsqrt(jnp.maximum(square, 1e-30))
    inner = TAU_ZERO * TAU_ZERO + (18.0 * math.sqrt(2.0) * SMAGORINSKY * SMAGORINSKY / 9.0) * magnitude
    rate = 2.0 * reciprocal(TAU_ZERO + inner * lax.rsqrt(inner))
    keep = 1.0 - rate
    weight = (rate * density) * (1.0 / 36.0)
    bx, by, bz = weight * vx, weight * vy, weight * vz
    axx, ayy, azz = weight * vxx, weight * vyy, weight * vzz
    hx, hy, hz = 0.5 * axx, 0.5 * ayy, 0.5 * azz
    base = weight - (hx + hy + hz) * (1.0 / 3.0)
    double = base + base
    out = [None] * POPS
    out[0] = keep * f[0] + 12.0 * base
    for index, even, odd in ((1, double + axx, bx + bx), (3, double + ayy, by + by), (5, double + azz, bz + bz)):
        out[index] = keep * f[index] + (even + odd)
        out[index + 1] = keep * f[index + 1] + (even - odd)
    for index, first, second, half_first, half_second, mixed in (
        (7, bx, by, hx, hy, weight * vxy),
        (11, bx, bz, hx, hz, weight * vxz),
        (15, by, bz, hy, hz, weight * vyz),
    ):
        middle = base + (half_first + half_second)
        same, other = middle + mixed, middle - mixed
        plus, minus = first + second, first - second
        out[index] = keep * f[index] + (same + plus)
        out[index + 1] = keep * f[index + 1] + (same - plus)
        out[index + 2] = keep * f[index + 2] + (other + minus)
        out[index + 3] = keep * f[index + 3] + (other - minus)
    return out


def kernel(
    spans,
    streams,
    populations,
    camera_in,
    active_in,
    order_in,
    final,
    tile_image,
    camera,
    active_list,
    tile_order,
    field,
    post0,
    post1,
    post2,
    speed,
    strips,
    speed_strips,
    rims,
    arrived,
    speed_rims,
    foot,
    outgoing,
    incoming,
    send_sem,
    recv_sem,
    load_sem,
    own_sem,
    small_sem,
):
    stream = lax.axis_index("stream")
    span = lax.axis_index("span")
    stream_up = lax.rem(stream + 1, streams)
    stream_down = lax.rem(stream + streams - 1, streams)
    span_up = lax.rem(span + 1, spans)
    span_down = lax.rem(span + spans - 1, spans)
    span_far = lax.rem(span + 2, spans)

    barrier = pltpu.get_barrier_semaphore()
    partners = (
        (stream_up, span),
        (stream_down, span),
        (stream, span_up),
        (stream, span_down),
        (stream_up, span_up),
        (stream_up, span_down),
        (stream_down, span_up),
        (stream_down, span_down),
        (stream, span_far),
    )
    for partner in partners:
        pl.semaphore_signal(barrier, inc=1, device_id=partner, device_id_type=MESH)

    loads = [None] * COLUMNS
    for k in range(COLUMNS // 2):
        for column in (k, COLUMNS - 1 - k):
            loads[column] = pltpu.make_async_copy(
                populations.at[:, :, pl.ds(column * LANES, LANES)], field.at[:, column], load_sem.at[column]
            )
            loads[column].start()
    small = [
        pltpu.make_async_copy(source, target, small_sem.at[number])
        for number, (source, target) in enumerate(
            ((camera_in, camera), (active_in, active_list), (order_in, tile_order))
        )
    ]
    for copy in small:
        copy.start()

    lane = lax.broadcasted_iota(jnp.int32, (8, LANES), 1)
    upper = lane >= NZ
    level = lax.rem(lane, NZ)
    floor = level == 0
    ceiling = level == NZ - 1

    def remote(source, target, number, device):
        return pltpu.make_async_remote_copy(
            src_ref=source,
            dst_ref=target,
            send_sem=send_sem.at[number],
            recv_sem=recv_sem.at[number],
            device_id=device,
            device_id_type=MESH,
        )

    before_row, after_row = TOP - 1, TOP + PLANES
    before_place, after_place = 0, PLACES - 1

    def x_copies(buffer, strip, up, down, number):
        places = pl.ds(1, COLUMNS)
        return [
            remote(strip.at[0], buffer.at[pl.ds(*up), places, before_row], number, (stream_up, span)),
            remote(strip.at[1], buffer.at[pl.ds(*down), places, after_row], number + 1, (stream_down, span)),
        ]

    def y_copies(up_source, up_target, down_source, down_target, number):
        return [
            remote(up_source, up_target, number, (stream, span_up)),
            remote(down_source, down_target, number + 1, (stream, span_down)),
        ]

    def corner_copies(buffer, strip, number):
        copies = []
        for index, side, column, place, row, device in (
            (7, 0, COLUMNS - 1, before_place, before_row, (stream_up, span_up)),
            (9, 0, 0, after_place, before_row, (stream_up, span_down)),
            (10, 1, COLUMNS - 1, before_place, after_row, (stream_down, span_up)),
            (8, 1, 0, after_place, after_row, (stream_down, span_down)),
        ):
            first = (X_UP, X_DOWN)[side][0]
            copies.append(
                remote(
                    strip.at[side, SLOT[index] - first, pl.ds(column, 1)],
                    buffer.at[SLOT[index], place, pl.ds(row, 1)],
                    number + len(copies),
                    device,
                )
            )
        return copies

    def joined(along_y, before, here, after):
        if along_y == 1:
            return jnp.where(upper, before(), here())
        if along_y == -1:
            return jnp.where(upper, here(), after())
        return here()

    def block_reader(buffer, place, block):
        def read(slot, along_y, plane):
            rows = pl.ds(TOP + 8 * block + plane, 8)
            return joined(
                along_y,
                lambda: buffer[slot, place - 1, rows],
                lambda: buffer[slot, place, rows],
                lambda: buffer[slot, place + 1, rows],
            )

        return read

    def strip_reader(buffer, plane, half):
        flat = buffer.reshape(buffer.shape[0], PLACES * ROWS, LANES)
        first = (8 * half + 1) * ROWS + TOP + plane

        def read(slot, along_y, along):
            def at(step):
                return lambda: flat[slot, pl.ds(first + step * ROWS + along, 8, stride=ROWS)]

            return joined(along_y, at(-1), at(0), at(1))

        return read

    def rim_reader(buffer, block):
        def read(slot, along_y, plane):
            rows = pl.ds(TOP + 8 * block + plane, 8)
            high, low = {0: (COLUMNS, 1), 1: (0, COLUMNS), -1: (1, PLACES - 1)}[along_y]
            return jnp.where(upper, buffer[slot, high, rows], buffer[slot, low, rows])

        return read

    def streamed(read):
        values = []
        for index in range(POPS):
            along_x, along_y, along_z = VELOCITIES[index]
            value = read(SLOT[index], along_y, -along_x)
            shift = ((NZ if along_y else 0) + along_z) % LANES
            if shift:
                value = pltpu.roll(value, shift, 1)
            if along_z:
                value = jnp.where(
                    floor if along_z > 0 else ceiling, read(SLOT[OPPOSITE[index]], 0, 0), value
                )
            values.append(value)
        return values

    def all_columns(work):
        def body(k, carry):
            work(2 * k)
            work(2 * k + 1)
            return carry

        lax.fori_loop(0, COLUMNS // 2, body, 0)

    sent = []

    def send(copies):
        for copy in copies:
            copy.start()
        sent.extend(copies)

    buffers = (post0, post1, post2)
    x_sides = [
        x_copies(buffer, strips.at[phase], X_UP, X_DOWN, phase * POST_MESSAGES)
        for phase, buffer in enumerate(buffers)
    ]
    corners = [
        corner_copies(buffer, strips.at[phase], phase * POST_MESSAGES + 2) for phase, buffer in enumerate(buffers)
    ]
    y_sides = [
        y_copies(
            rims.at[phase, 0],
            arrived.at[phase, 0],
            rims.at[phase, 1],
            arrived.at[phase, 1],
            phase * POST_MESSAGES + 6,
        )
        for phase in range(3)
    ]

    def post_strips(phase, values_of):
        for side, (first, count) in enumerate((X_UP, X_DOWN)):
            for half in range(2):
                out = collide(values_of((PLANES - 1, 0)[side], half))
                for place in range(count):
                    strips[phase, side, place, pl.ds(8 * half, 8)] = out[ORDER[first + place]]

    def post_rims(phase, values_of):
        for block in range(BLOCKS):
            out = collide(values_of(block))
            rows = pl.ds(8 * block, 8)
            for side in range(2):
                for pack, (first, second) in enumerate(Y_PACKS[side]):
                    value = out[first]
                    if second is not None:
                        other = pltpu.roll(out[second], NZ, 1)
                        value = jnp.where(upper, other, value) if side else jnp.where(upper, value, other)
                    rims[phase, side, pack, rows] = value

    def await_rims(phase):
        for copy in x_sides[phase] + corners[phase] + y_sides[phase]:
            copy.wait_recv()
        for side, place in enumerate((before_place, after_place)):
            for pack, (first, second) in enumerate(Y_PACKS[side]):
                for block in range(BLOCKS):
                    value = arrived[phase, side, pack, pl.ds(8 * block, 8)]
                    rows = pl.ds(TOP + 8 * block, 8)
                    buffers[phase][SLOT[first], place, rows] = value
                    if second is not None:
                        buffers[phase][SLOT[second], place, rows] = pltpu.roll(value, NZ, 1)

    def post_column(target, column, values_of):
        for block in range(BLOCKS):
            out = collide(values_of(block))
            for index in range(POPS):
                target[SLOT[index], column + 1, pl.ds(TOP + 8 * block, 8)] = out[index]

    def first_work(column):
        post_column(
            post0,
            column,
            lambda block: [field[index, column, pl.ds(8 * block, 8)] for index in range(POPS)],
        )

    for column in (0, COLUMNS - 1):
        loads[column].wait()
    post_rims(
        0,
        lambda block: [
            jnp.where(upper, field[index, COLUMNS - 1, pl.ds(8 * block, 8)], field[index, 0, pl.ds(8 * block, 8)])
            for index in range(POPS)
        ],
    )
    for column in range(1, COLUMNS - 1):
        loads[column].wait()
    flat_field = field.reshape(POPS, COLUMNS * PLANES, LANES)
    post_strips(
        0,
        lambda plane, half: [
            flat_field[index, pl.ds(8 * half * PLANES + plane, 8, stride=PLANES)] for index in range(POPS)
        ],
    )
    pl.semaphore_wait(barrier, len(partners))
    send(x_sides[0] + corners[0] + y_sides[0])
    all_columns(first_work)

    for phase in (1, 2):
        source, target = buffers[phase - 1], buffers[phase]
        await_rims(phase - 1)
        post_strips(phase, lambda plane, half: streamed(strip_reader(source, plane, half)))
        send(x_sides[phase] + corners[phase])
        post_rims(phase, lambda block: streamed(rim_reader(source, block)))
        send(y_sides[phase])

        def step_work(column):
            post_column(target, column, lambda block: streamed(block_reader(source, column + 1, block)))

        all_columns(step_work)

    def velocity(values):
        _, flow, _, _, density = moments(values)
        inverse = reciprocal(density)
        return [part * inverse for part in flow]

    def last_work(column):
        lanes = pl.ds(pl.multiple_of(column * LANES, LANES), LANES)
        for block in range(BLOCKS):
            values = streamed(block_reader(post2, column + 1, block))
            for index in range(POPS):
                final[index, pl.ds(8 * block, 8), lanes] = values[index]
            for dimension, part in enumerate(velocity(values)):
                speed[dimension, column + 1, pl.ds(TOP + 8 * block, 8)] = part

    await_rims(2)
    for side in range(2):
        for half in range(2):
            values = streamed(strip_reader(post2, (PLANES - 1, 0)[side], half))
            for dimension, part in enumerate(velocity(values)):
                speed_strips[side, dimension, pl.ds(8 * half, 8)] = part
    speed_x = x_copies(speed, speed_strips, (0, 3), (0, 3), SPEED_BASE)
    send(speed_x)
    for block in range(BLOCKS):
        for dimension, part in enumerate(velocity(streamed(rim_reader(post2, block)))):
            speed_rims[dimension, pl.ds(8 * block, 8)] = part
    rows = pl.ds(TOP, PLANES)
    speed_y = y_copies(
        speed_rims, speed.at[:, before_place, rows], speed_rims, speed.at[:, after_place, rows], SPEED_BASE + 2
    )
    send(speed_y)
    all_columns(last_work)

    for copy in small:
        copy.wait()

    bits = jnp.int32(0)
    for entry in range(32):
        number = active_list[entry]
        bits = bits | jnp.where(number < 32, jnp.left_shift(jnp.int32(1), jnp.minimum(number, 31)), 0)
    falling = jnp.full((8, LANES), camera[0], jnp.int32) == 1
    leading = falling == upper
    bits = jnp.full((8, LANES), bits, jnp.int32)
    corner = 4 * (lax.broadcasted_iota(jnp.int32, (8, LANES), 0) // 4)

    def ray(k, side, block, sums):
        column = k if side == 0 else COLUMNS - 1 - k
        read = block_reader(speed, column + 1, block)
        centre = [read(dimension, 0, 0) for dimension in range(3)]
        slope_x, slope_y, slope_z = [], [], []
        for dimension in range(3):
            here = centre[dimension]
            slope_x.append(read(dimension, 0, 1) - read(dimension, 0, -1))
            slope_y.append(pltpu.roll(read(dimension, -1, 0) - read(dimension, 1, 0), NZ, 1))
            above = jnp.where(ceiling, -here, pltpu.roll(here, LANES - 1, 1))
            below = jnp.where(floor, -here, pltpu.roll(here, 1, 1))
            slope_z.append(above - below)
        cross = slope_x[1] * slope_y[0] + slope_x[2] * slope_z[0] + slope_y[2] * slope_z[1]
        total = slope_x[0] * slope_x[0] + slope_y[1] * slope_y[1] + slope_z[2] * slope_z[2] + (cross + cross)
        vortex = total * (-0.125 / VORTEX_SCALE)
        small = jnp.exp(-jnp.abs(vortex))
        one = 1.0 + small
        share = reciprocal(one)
        colours = [jnp.where(vortex >= 0.0, share, small * share)]
        for dimension in (0, 2):
            colours.append(reciprocal(1.0 + jnp.exp(centre[dimension] * (-1.0 / SPEED_SCALE))))
        passing = jnp.exp(-OPACITY_GAIN * (jnp.maximum(vortex, 0.0) + jnp.log(one)))
        brick = corner + (8 * block + column // 4)
        passing = jnp.where((jnp.right_shift(bits, brick) & 1) == 1, passing, 1.0)
        opacity = 1.0 - passing
        other = pltpu.roll(passing, NZ, 1)
        both = passing * other
        weight = opacity * jnp.where(leading, 1.0, other)
        from_back = falling if side == 1 else jnp.logical_not(falling)
        through = sums[3]
        weight = weight * jnp.where(from_back, 1.0, through)
        fade = jnp.where(from_back, both, 1.0)
        return tuple(sums[n] * fade + colours[n] * weight for n in range(3)) + (through * both,)

    start = tuple(jnp.zeros((8, LANES), jnp.float32) for _ in range(3)) + (jnp.ones((8, LANES), jnp.float32),)
    sums = {(side, block): start for side in range(2) for block in range(BLOCKS)}

    def walk(blocks):
        keys = [(side, block) for side in range(2) for block in blocks]

        def body(step, carry):
            k = COLUMNS // 2 - 1 - step
            return tuple(ray(k, side, block, carry[n]) for n, (side, block) in enumerate(keys))

        out = lax.fori_loop(0, COLUMNS // 2 - 1, body, tuple(sums[key] for key in keys))
        sums.update(zip(keys, out))

    walk((1, 2))
    for copy in speed_x:
        copy.wait_recv()
    walk((0, 3))
    for copy in speed_y:
        copy.wait_recv()
    for key in sums:
        sums[key] = ray(0, key[0], key[1], sums[key])

    for block in range(BLOCKS):
        low, high = sums[0, block], sums[1, block]
        front = [jnp.where(falling, b, a) for a, b in zip(low, high)]
        back = [jnp.where(falling, a, b) for a, b in zip(low, high)]
        for number in range(4):
            if number < 3:
                half = front[number] + front[3] * back[number]
                value = half + pltpu.roll(half, NZ, 1)
            else:
                value = front[3] * back[3]
            for part in range(2):
                foot[2 * block + part, pl.ds(4 * number, 4)] = value[4 * part : 4 * part + 4]

    for number in range(8):
        outgoing[number] = foot[tile_order[number]]
    tiles = []
    for hop, target in enumerate((span_up, span_down, span_far)):
        tiles.append(
            remote(
                outgoing.at[pl.ds(2 * target, 2)], incoming.at[span], TILE_BASE + hop, (stream, target)
            )
        )
    send(tiles)
    own = pltpu.make_async_copy(outgoing.at[pl.ds(2 * span, 2)], incoming.at[span], own_sem)
    own.start()
    own.wait()
    for copy in tiles:
        copy.wait_recv()
    wide = jnp.broadcast_to(camera[0], (16, LANES)) == 1
    upper_row = lax.broadcasted_iota(jnp.int32, (1, LANES), 1) >= NZ
    for tile in range(2):
        sheets = [incoming[source, tile] for source in range(spans)]
        colour = sheets[0][:12]
        through = sheets[0][12:]
        for source in range(1, spans):
            sheet = sheets[source]
            fade = jnp.concatenate([sheet[12:]] * 3, axis=0)
            veil = jnp.concatenate([through] * 3, axis=0)
            colour = jnp.where(wide[:12], colour * fade + sheet[:12], colour + veil * sheet[:12])
            through = through * sheet[12:]
        for number in range(4):
            quad = colour[4 * number : 4 * number + 4] if number < 3 else through
            for part in range(2):
                tile_image[tile, pl.ds(number, 1), pl.ds(part * LANES, LANES)] = jnp.where(
                    upper_row, quad[2 * part + 1 : 2 * part + 2], quad[2 * part : 2 * part + 1]
                )

    for copy in sent:
        copy.wait_send()


def store_kernel(final, tile_image, final_out, image_out, sems):
    copies = [
        pltpu.make_async_copy(final.at[index], final_out.at[index], sems.at[index]) for index in range(POPS)
    ]
    copies.append(pltpu.make_async_copy(tile_image, image_out, sems.at[POPS]))
    for copy in copies:
        copy.start()
    for copy in copies:
        copy.wait()


def on_device(populations, camera, active_list, tile_order):
    spans = lax.axis_size("span")
    streams = lax.axis_size("stream")
    vmem = functools.partial(pl.BlockSpec, memory_space=pltpu.VMEM)
    pinned = functools.partial(pltpu.with_memory_space_constraint, memory_space=pltpu.HBM)
    anywhere = functools.partial(pl.BlockSpec, memory_space=pl.ANY)
    post = pltpu.VMEM((POPS, PLACES, ROWS, LANES), jnp.float32)
    final, tile_image = pl.pallas_call(
        functools.partial(kernel, spans, streams),
        out_shape=(
            jax.ShapeDtypeStruct(populations.shape, jnp.float32),
            jax.ShapeDtypeStruct((2, 4, 256), jnp.float32),
        ),
        in_specs=[anywhere()] * 4,
        out_specs=(vmem(), vmem()),
        scratch_shapes=[
            pltpu.SMEM(camera.shape, jnp.int32),
            pltpu.SMEM((active_list.size,), jnp.int32),
            pltpu.SMEM((tile_order.size,), jnp.int32),
            pltpu.VMEM((POPS, COLUMNS, PLANES, LANES), jnp.float32),
            post,
            post,
            post,
            pltpu.VMEM((3, PLACES, ROWS, LANES), jnp.float32),
            pltpu.VMEM((3, 2, 5, COLUMNS, LANES), jnp.float32),
            pltpu.VMEM((2, 3, COLUMNS, LANES), jnp.float32),
            pltpu.VMEM((3, 2, 3, PLANES, LANES), jnp.float32),
            pltpu.VMEM((3, 2, 3, PLANES, LANES), jnp.float32),
            pltpu.VMEM((3, PLANES, LANES), jnp.float32),
            pltpu.VMEM((8, 16, LANES), jnp.float32),
            pltpu.VMEM((8, 16, LANES), jnp.float32),
            pltpu.VMEM((spans, 2, 16, LANES), jnp.float32),
            pltpu.SemaphoreType.DMA((MESSAGES,)),
            pltpu.SemaphoreType.DMA((MESSAGES,)),
            pltpu.SemaphoreType.DMA((COLUMNS,)),
            pltpu.SemaphoreType.DMA,
            pltpu.SemaphoreType.DMA((3,)),
        ],
        compiler_params=pltpu.CompilerParams(
            collective_id=0, has_side_effects=True, vmem_limit_bytes=48 * 1024 * 1024
        ),
    )(populations, camera, pinned(active_list.reshape(-1)), pinned(tile_order.reshape(-1)))
    return pl.pallas_call(
        store_kernel,
        out_shape=(
            jax.ShapeDtypeStruct(final.shape, jnp.float32),
            jax.ShapeDtypeStruct(tile_image.shape, jnp.float32),
        ),
        in_specs=[anywhere()] * 2,
        out_specs=(anywhere(), anywhere()),
        scratch_shapes=[pltpu.SemaphoreType.DMA((POPS + 1,))],
        compiler_params=pltpu.CompilerParams(vmem_limit_bytes=1024 * 1024),
    )(final, tile_image)


def solution(mesh):
    placed = (P(None, "stream", "span"), P("stream"), P("stream", "span", None), P("stream", None))
    return jax.shard_map(
        on_device,
        mesh=mesh,
        in_specs=placed,
        out_specs=(P(None, "stream", "span"), P(("stream", "span"), None, None)),
        check_vma=False,
    )
```

```python
import functools
import math

import jax
import jax.numpy as jnp
from jax import lax
from jax.experimental import pallas as pl
from jax.experimental.pallas import tpu as pltpu
from jax.sharding import PartitionSpec as P

MESH = pl.DeviceIdType.MESH

NZ = 64
LANES = 128
POPS = 19
PLANES = 32
COLUMNS = 16
TOP = 8
ROWS = 48
BLOCKS = PLANES // 8

VELOCITIES = (
    (0, 0, 0),
    (1, 0, 0),
    (-1, 0, 0),
    (0, 1, 0),
    (0, -1, 0),
    (0, 0, 1),
    (0, 0, -1),
    (1, 1, 0),
    (-1, -1, 0),
    (1, -1, 0),
    (-1, 1, 0),
    (1, 0, 1),
    (-1, 0, -1),
    (1, 0, -1),
    (-1, 0, 1),
    (0, 1, 1),
    (0, -1, -1),
    (0, 1, -1),
    (0, -1, 1),
)
OPPOSITE = (0, 2, 1, 4, 3, 6, 5, 8, 7, 10, 9, 12, 11, 14, 13, 16, 15, 18, 17)
TAU_ZERO = 0.55
SMAGORINSKY = 0.17
VORTEX_SCALE = 0.003
SPEED_SCALE = 0.08
OPACITY_GAIN = 0.03

ORDER = (1, 11, 13, 9, 7, 3, 15, 17, 0, 5, 6, 4, 16, 18, 10, 2, 12, 14, 8)
SLOT = tuple(ORDER.index(index) for index in range(POPS))
X_UP, NOT_UP = (0, 5), (5, 14)
X_DOWN, NOT_DOWN = (14, 5), (0, 14)
Y_PACKS = (((7, 3), (15, 17), (10, None)), ((8, 4), (16, 18), (9, None)))

PLACES = COLUMNS + 2
POST_MESSAGES = 8
SPEED_BASE = 3 * POST_MESSAGES
LATE_BASE = SPEED_BASE + 2
TILE_BASE = LATE_BASE + 12
MESSAGES = TILE_BASE + 3


def reciprocal(value):
    return pl.reciprocal(value, approx=True)


def moments(f):
    pair = {index: f[index] + f[index + 1] for index in range(1, POPS, 2)}
    gap = {index: f[index] - f[index + 1] for index in range(1, POPS, 2)}
    flow = (
        (gap[1] + gap[7]) + (gap[9] + gap[11]) + gap[13],
        (gap[3] + gap[7]) + (gap[15] - gap[9]) + gap[17],
        (gap[5] + gap[11]) + (gap[15] - gap[13]) - gap[17],
    )
    around_xy = pair[7] + pair[9]
    around_xz = pair[11] + pair[13]
    around_yz = pair[15] + pair[17]
    along_x = pair[1] + (around_xy + around_xz)
    density = (f[0] + pair[3]) + (pair[5] + around_yz) + along_x
    return pair, flow, (around_xy, around_xz, around_yz), along_x, density


def collide(f):
    pair, flow, around, along_x, density = moments(f)
    along_y = pair[3] + (around[0] + around[2])
    along_z = pair[5] + (around[1] + around[2])
    inverse = reciprocal(density)
    triple = 3.0 * inverse
    ninth = 9.0 * inverse
    vx, vy, vz = [part * triple for part in flow]
    vxx, vyy, vzz = vx * vx, vy * vy, vz * vz
    vxy, vxz, vyz = vx * vy, vx * vz, vy * vz
    qxx = ninth * along_x - (3.0 + vxx)
    qyy = ninth * along_y - (3.0 + vyy)
    qzz = ninth * along_z - (3.0 + vzz)
    qxy = ninth * (pair[7] - pair[9]) - vxy
    qxz = ninth * (pair[11] - pair[13]) - vxz
    qyz = ninth * (pair[15] - pair[17]) - vyz
    cross = qxy * qxy + qxz * qxz + qyz * qyz
    square = (qxx * qxx + qyy * qyy) + (qzz * qzz + (cross + cross))
    magnitude = square * lax.rsqrt(jnp.maximum(square, 1e-30))
    inner = TAU_ZERO * TAU_ZERO + (18.0 * math.sqrt(2.0) * SMAGORINSKY * SMAGORINSKY / 9.0) * magnitude
    rate = 2.0 * reciprocal(TAU_ZERO + inner * lax.rsqrt(inner))
    keep = 1.0 - rate
    weight = (rate * density) * (1.0 / 36.0)
    bx, by, bz = weight * vx, weight * vy, weight * vz
    half = 0.5 * weight
    ax, ay, az = half * vxx, half * vyy, half * vzz
    base = weight - (ax + ay + az) * (1.0 / 3.0)
    ex, ey, ez = base + ax, base + ay, base + az
    out = [None] * POPS
    out[0] = keep * f[0] + 12.0 * base
    for index, even, odd in ((1, ex, bx), (3, ey, by), (5, ez, bz)):
        out[index] = keep * f[index] + 2.0 * (even + odd)
        out[index + 1] = keep * f[index + 1] + 2.0 * (even - odd)
    for index, first, second, middle, mixed in (
        (7, bx, by, ex + ay, weight * vxy),
        (11, bx, bz, ex + az, weight * vxz),
        (15, by, bz, ey + az, weight * vyz),
    ):
        same, other = middle + mixed, middle - mixed
        plus, minus = first + second, first - second
        out[index] = keep * f[index] + (same + plus)
        out[index + 1] = keep * f[index + 1] + (same - plus)
        out[index + 2] = keep * f[index + 2] + (other + minus)
        out[index + 3] = keep * f[index + 3] + (other - minus)
    return out


def kernel(
    spans,
    streams,
    populations,
    camera_in,
    active_in,
    order_in,
    final,
    tile_image,
    camera,
    active_list,
    tile_order,
    field,
    post0,
    post1,
    post2,
    speed,
    strips,
    deep,
    second,
    rims,
    arrived,
    speed_rims,
    foot,
    outgoing,
    incoming,
    send_sem,
    recv_sem,
    load_sem,
    own_sem,
    small_sem,
):
    stream = lax.axis_index("stream")
    span = lax.axis_index("span")
    stream_up = lax.rem(stream + 1, streams)
    stream_down = lax.rem(stream + streams - 1, streams)
    span_up = lax.rem(span + 1, spans)
    span_down = lax.rem(span + spans - 1, spans)
    span_far = lax.rem(span + 2, spans)

    barrier = pltpu.get_barrier_semaphore()
    partners = (
        (stream_up, span),
        (stream_down, span),
        (stream, span_up),
        (stream, span_down),
        (stream_up, span_up),
        (stream_up, span_down),
        (stream_down, span_up),
        (stream_down, span_down),
        (stream, span_far),
    )
    for partner in partners:
        pl.semaphore_signal(barrier, inc=1, device_id=partner, device_id_type=MESH)

    loads = [None] * COLUMNS
    for k in range(COLUMNS // 2):
        for column in (k, COLUMNS - 1 - k):
            loads[column] = pltpu.make_async_copy(
                populations.at[:, :, pl.ds(column * LANES, LANES)], field.at[:, column], load_sem.at[column]
            )
            loads[column].start()
    small = [
        pltpu.make_async_copy(source, target, small_sem.at[number])
        for number, (source, target) in enumerate(
            ((camera_in, camera), (active_in, active_list), (order_in, tile_order))
        )
    ]
    for copy in small:
        copy.start()

    lane = lax.broadcasted_iota(jnp.int32, (8, LANES), 1)
    upper = lane >= NZ
    level = lax.rem(lane, NZ)
    floor = level == 0
    ceiling = level == NZ - 1

    def remote(source, target, number, device):
        return pltpu.make_async_remote_copy(
            src_ref=source,
            dst_ref=target,
            send_sem=send_sem.at[number],
            recv_sem=recv_sem.at[number],
            device_id=device,
            device_id_type=MESH,
        )

    before_row, after_row = TOP - 1, TOP + PLANES
    before_place, after_place = 0, PLACES - 1

    def x_copies(buffer, up_strip, down_strip, up, down, depth, number):
        places = pl.ds(1, COLUMNS)
        return [
            remote(up_strip, buffer.at[pl.ds(*up), places, before_row - depth], number, (stream_up, span)),
            remote(down_strip, buffer.at[pl.ds(*down), places, after_row + depth], number + 1, (stream_down, span)),
        ]

    def y_copies(up_source, up_target, down_source, down_target, number):
        return [
            remote(up_source, up_target, number, (stream, span_up)),
            remote(down_source, down_target, number + 1, (stream, span_down)),
        ]

    corner_paths = (
        (7, 0, COLUMNS - 1, before_place, before_row, (stream_up, span_up)),
        (9, 0, 0, after_place, before_row, (stream_up, span_down)),
        (10, 1, COLUMNS - 1, before_place, after_row, (stream_down, span_up)),
        (8, 1, 0, after_place, after_row, (stream_down, span_down)),
    )

    def corner_copies(buffer, strip, number, first, count=1, depth=0):
        copies = []
        for index, side, column, place, row, device in corner_paths:
            slot = SLOT[index] if count == 1 else SLOT[3 if column else 4]
            outwards = -depth if row == before_row else depth
            copies.append(
                remote(
                    strip[side].at[pl.ds(slot - first[side], count), pl.ds(column, 1)],
                    buffer.at[pl.ds(slot, count), place, pl.ds(row + outwards, 1)],
                    number + len(copies),
                    device,
                )
            )
        return copies

    def joined(along_y, before, here, after):
        if along_y == 1:
            return jnp.where(upper, before(), here())
        if along_y == -1:
            return jnp.where(upper, here(), after())
        return here()

    def block_reader(buffer, place, block):
        def read(slot, along_y, plane):
            rows = pl.ds(TOP + 8 * block + plane, 8)
            return joined(
                along_y,
                lambda: buffer[slot, place - 1, rows],
                lambda: buffer[slot, place, rows],
                lambda: buffer[slot, place + 1, rows],
            )

        return read

    def strip_reader(buffer, plane, half):
        flat = buffer.reshape(buffer.shape[0], PLACES * ROWS, LANES)
        first = (8 * half + 1) * ROWS + TOP + plane

        def read(slot, along_y, along):
            def at(step):
                return lambda: flat[slot, pl.ds(first + step * ROWS + along, 8, stride=ROWS)]

            return joined(along_y, at(-1), at(0), at(1))

        return read

    def rim_reader(buffer, block):
        def read(slot, along_y, plane):
            rows = pl.ds(TOP + 8 * block + plane, 8)
            high, low = {0: (COLUMNS, 1), 1: (0, COLUMNS), -1: (1, PLACES - 1)}[along_y]
            return jnp.where(upper, buffer[slot, high, rows], buffer[slot, low, rows])

        return read

    def streamed(read):
        values = []
        for index in range(POPS):
            along_x, along_y, along_z = VELOCITIES[index]
            value = read(SLOT[index], along_y, -along_x)
            shift = ((NZ if along_y else 0) + along_z) % LANES
            if shift:
                value = pltpu.roll(value, shift, 1)
            if along_z:
                value = jnp.where(
                    floor if along_z > 0 else ceiling, read(SLOT[OPPOSITE[index]], 0, 0), value
                )
            values.append(value)
        return values

    def sweep(work, first, last, step, blocks):
        def body(k, carry):
            for part in range(step):
                work(first + step * k + part, blocks)
            return carry

        lax.fori_loop(0, (last - first) // step, body, 0)

    everything = tuple(range(BLOCKS))

    def inner(work):
        sweep(work, 1, COLUMNS - 1, 7, (1, 2))

    def outer(work):
        for column in (0, COLUMNS - 1):
            work(column, (1, 2))
        sweep(work, 0, COLUMNS, 8, (0, 3))

    sent = []

    def send(copies):
        for copy in copies:
            copy.start()
        sent.extend(copies)

    buffers = (post0, post1, post2)
    edge_strips = [(strips.at[phase, 0], strips.at[phase, 1]) for phase in range(2)]
    edge_strips.append((deep.at[0, pl.ds(*X_UP)], deep.at[1, pl.ds(*X_DOWN)]))
    x_sides, corners = [], []
    for phase, buffer in enumerate(buffers):
        number = phase * POST_MESSAGES
        x_sides.append(x_copies(buffer, *edge_strips[phase], X_UP, X_DOWN, 0, number))
        if phase < 2:
            corners.append(
                corner_copies(buffer, edge_strips[phase], number + 2, (X_UP[0], X_DOWN[0]))
            )
        else:
            corners.append(corner_copies(buffer, (deep.at[0], deep.at[1]), number + 2, (0, 0)))
    late = x_copies(
        post2, deep.at[0, pl.ds(*NOT_UP)], deep.at[1, pl.ds(*NOT_DOWN)], NOT_UP, NOT_DOWN, 0, LATE_BASE
    )
    late += x_copies(post2, second.at[0], second.at[1], X_UP, X_DOWN, 1, LATE_BASE + 2)
    late += corner_copies(post2, (deep.at[0], deep.at[1]), LATE_BASE + 4, (0, 0), count=3)
    late += corner_copies(
        post2, (second.at[0], second.at[1]), LATE_BASE + 8, (X_UP[0], X_DOWN[0]), depth=1
    )
    y_sides = [
        y_copies(
            rims.at[phase, 0],
            arrived.at[phase, 0],
            rims.at[phase, 1],
            arrived.at[phase, 1],
            phase * POST_MESSAGES + 6,
        )
        for phase in range(3)
    ]

    def post_strips(values_of, planes, store):
        for side in range(2):
            for half in range(2):
                out = collide(values_of(planes[side], half))
                store(side, pl.ds(8 * half, 8), out)

    def store_edges(phase):
        def store(side, rows, out):
            first, count = (X_UP, X_DOWN)[side]
            for place in range(count):
                strips[phase, side, place, rows] = out[ORDER[first + place]]

        return store

    def store_deep(side, rows, out):
        for index in range(POPS):
            deep[side, SLOT[index], rows] = out[index]

    def store_second(side, rows, out):
        first, count = (X_UP, X_DOWN)[side]
        for place in range(count):
            second[side, place, rows] = out[ORDER[first + place]]

    edge_planes, second_planes = (PLANES - 1, 0), (PLANES - 2, 1)

    def post_rims(phase, values_of):
        for block in range(BLOCKS):
            out = collide(values_of(block))
            rows = pl.ds(8 * block, 8)
            for side in range(2):
                for pack, (first, second) in enumerate(Y_PACKS[side]):
                    value = out[first]
                    if second is not None:
                        other = pltpu.roll(out[second], NZ, 1)
                        value = jnp.where(upper, other, value) if side else jnp.where(upper, value, other)
                    rims[phase, side, pack, rows] = value

    def await_rims(phase):
        for copy in x_sides[phase] + corners[phase] + y_sides[phase]:
            copy.wait_recv()
        for side, place in enumerate((before_place, after_place)):
            for pack, (first, second) in enumerate(Y_PACKS[side]):
                for block in range(BLOCKS):
                    value = arrived[phase, side, pack, pl.ds(8 * block, 8)]
                    rows = pl.ds(TOP + 8 * block, 8)
                    buffers[phase][SLOT[first], place, rows] = value
                    if second is not None:
                        buffers[phase][SLOT[second], place, rows] = pltpu.roll(value, NZ, 1)

    def post_column(target, column, blocks, values_of):
        for block in blocks:
            out = collide(values_of(block))
            for index in range(POPS):
                target[SLOT[index], column + 1, pl.ds(TOP + 8 * block, 8)] = out[index]

    def first_work(column, blocks):
        post_column(
            post0,
            column,
            blocks,
            lambda block: [field[index, column, pl.ds(8 * block, 8)] for index in range(POPS)],
        )

    for column in (0, COLUMNS - 1):
        loads[column].wait()
    post_rims(
        0,
        lambda block: [
            jnp.where(upper, field[index, COLUMNS - 1, pl.ds(8 * block, 8)], field[index, 0, pl.ds(8 * block, 8)])
            for index in range(POPS)
        ],
    )
    for column in range(1, COLUMNS - 1):
        loads[column].wait()
    flat_field = field.reshape(POPS, COLUMNS * PLANES, LANES)
    post_strips(
        lambda plane, half: [
            flat_field[index, pl.ds(8 * half * PLANES + plane, 8, stride=PLANES)] for index in range(POPS)
        ],
        edge_planes,
        store_edges(0),
    )
    pl.semaphore_wait(barrier, len(partners))
    send(x_sides[0] + corners[0] + y_sides[0])
    sweep(first_work, 0, COLUMNS, 4, everything)

    for phase in (1, 2):
        source, target = buffers[phase - 1], buffers[phase]

        def step_work(column, blocks):
            post_column(target, column, blocks, lambda block: streamed(block_reader(source, column + 1, block)))

        def strip_values(plane, half):
            return streamed(strip_reader(source, plane, half))

        inner(step_work)
        await_rims(phase - 1)
        post_strips(strip_values, edge_planes, store_edges(phase) if phase == 1 else store_deep)
        send(x_sides[phase] + corners[phase])
        post_rims(phase, lambda block: streamed(rim_reader(source, block)))
        send(y_sides[phase])
        if phase == 2:
            post_strips(strip_values, second_planes, store_second)
            send(late)
        outer(step_work)

    def velocity(values):
        _, flow, _, _, density = moments(values)
        inverse = reciprocal(density)
        return [part * inverse for part in flow]

    def last_work(column, blocks):
        lanes = pl.ds(pl.multiple_of(column * LANES, LANES), LANES)
        for block in blocks:
            values = streamed(block_reader(post2, column + 1, block))
            for index in range(POPS):
                final[index, pl.ds(8 * block, 8), lanes] = values[index]
            for dimension, part in enumerate(velocity(values)):
                speed[dimension, column + 1, pl.ds(TOP + 8 * block, 8)] = part

    inner(last_work)
    await_rims(2)
    for block in range(BLOCKS):
        for dimension, part in enumerate(velocity(streamed(rim_reader(post2, block)))):
            speed_rims[dimension, pl.ds(8 * block, 8)] = part
    rows = pl.ds(TOP, PLANES)
    speed_y = y_copies(
        speed_rims, speed.at[:, before_place, rows], speed_rims, speed.at[:, after_place, rows], SPEED_BASE
    )
    send(speed_y)
    outer(last_work)

    for copy in small:
        copy.wait()

    bits = jnp.int32(0)
    for entry in range(32):
        number = active_list[entry]
        bits = bits | jnp.where(number < 32, jnp.left_shift(jnp.int32(1), jnp.minimum(number, 31)), 0)
    falling = jnp.full((8, LANES), camera[0], jnp.int32) == 1
    leading = falling == upper
    bits = jnp.full((8, LANES), bits, jnp.int32)
    corner = 4 * (lax.broadcasted_iota(jnp.int32, (8, LANES), 0) // 4)

    def ray(k, side, block, sums):
        column = k if side == 0 else COLUMNS - 1 - k
        read = block_reader(speed, column + 1, block)
        centre = [read(dimension, 0, 0) for dimension in range(3)]
        slope_x, slope_y, slope_z = [], [], []
        for dimension in range(3):
            here = centre[dimension]
            slope_x.append(read(dimension, 0, 1) - read(dimension, 0, -1))
            slope_y.append(pltpu.roll(read(dimension, -1, 0) - read(dimension, 1, 0), NZ, 1))
            above = jnp.where(ceiling, -here, pltpu.roll(here, LANES - 1, 1))
            below = jnp.where(floor, -here, pltpu.roll(here, 1, 1))
            slope_z.append(above - below)
        cross = slope_x[1] * slope_y[0] + slope_x[2] * slope_z[0] + slope_y[2] * slope_z[1]
        total = slope_x[0] * slope_x[0] + slope_y[1] * slope_y[1] + slope_z[2] * slope_z[2] + (cross + cross)
        vortex = total * (-0.125 / VORTEX_SCALE)
        small = jnp.exp(-jnp.abs(vortex))
        one = 1.0 + small
        share = reciprocal(one)
        colours = [jnp.where(vortex >= 0.0, share, small * share)]
        for dimension in (0, 2):
            colours.append(reciprocal(1.0 + jnp.exp(centre[dimension] * (-1.0 / SPEED_SCALE))))
        passing = jnp.exp(-OPACITY_GAIN * (jnp.maximum(vortex, 0.0) + jnp.log(one)))
        brick = corner + (8 * block + column // 4)
        passing = jnp.where((jnp.right_shift(bits, brick) & 1) == 1, passing, 1.0)
        opacity = 1.0 - passing
        other = pltpu.roll(passing, NZ, 1)
        both = passing * other
        weight = opacity * jnp.where(leading, 1.0, other)
        from_back = falling if side == 1 else jnp.logical_not(falling)
        through = sums[3]
        weight = weight * jnp.where(from_back, 1.0, through)
        fade = jnp.where(from_back, both, 1.0)
        return tuple(sums[n] * fade + colours[n] * weight for n in range(3)) + (through * both,)

    start = tuple(jnp.zeros((8, LANES), jnp.float32) for _ in range(3)) + (jnp.ones((8, LANES), jnp.float32),)
    sums = {(side, block): start for side in range(2) for block in range(BLOCKS)}

    def walk(blocks):
        for k in range(COLUMNS // 2 - 1, 0, -1):
            for side in range(2):
                for block in blocks:
                    sums[side, block] = ray(k, side, block, sums[side, block])

    walk((1, 2))
    for copy in late:
        copy.wait_recv()
    flat_speed = speed.reshape(3, PLACES * ROWS, LANES)
    for plane in (-1, PLANES):
        for half in range(2):
            for dimension, part in enumerate(velocity(streamed(strip_reader(post2, plane, half)))):
                first = (8 * half + 1) * ROWS + TOP + plane
                flat_speed[dimension, pl.ds(first, 8, stride=ROWS)] = part
    walk((0, 3))
    for copy in speed_y:
        copy.wait_recv()
    for key in sums:
        sums[key] = ray(0, key[0], key[1], sums[key])

    for block in range(BLOCKS):
        low, high = sums[0, block], sums[1, block]
        front = [jnp.where(falling, b, a) for a, b in zip(low, high)]
        back = [jnp.where(falling, a, b) for a, b in zip(low, high)]
        for number in range(4):
            if number < 3:
                half = front[number] + front[3] * back[number]
                value = half + pltpu.roll(half, NZ, 1)
            else:
                value = front[3] * back[3]
            for part in range(2):
                foot[2 * block + part, pl.ds(4 * number, 4)] = value[4 * part : 4 * part + 4]

    for number in range(8):
        outgoing[number] = foot[tile_order[number]]
    tiles = []
    for hop, target in enumerate((span_up, span_down, span_far)):
        tiles.append(
            remote(
                outgoing.at[pl.ds(2 * target, 2)], incoming.at[span], TILE_BASE + hop, (stream, target)
            )
        )
    earlier = list(sent)
    send(tiles)
    own = pltpu.make_async_copy(outgoing.at[pl.ds(2 * span, 2)], incoming.at[span], own_sem)
    own.start()
    own.wait()
    for copy in earlier:
        copy.wait_send()
    for copy in tiles:
        copy.wait_recv()
    wide = jnp.broadcast_to(camera[0], (16, LANES)) == 1
    upper_row = lax.broadcasted_iota(jnp.int32, (1, LANES), 1) >= NZ
    for tile in range(2):
        sheets = [incoming[source, tile] for source in range(spans)]
        colour = sheets[0][:12]
        through = sheets[0][12:]
        for source in range(1, spans):
            sheet = sheets[source]
            fade = jnp.concatenate([sheet[12:]] * 3, axis=0)
            veil = jnp.concatenate([through] * 3, axis=0)
            colour = jnp.where(wide[:12], colour * fade + sheet[:12], colour + veil * sheet[:12])
            through = through * sheet[12:]
        for number in range(4):
            quad = colour[4 * number : 4 * number + 4] if number < 3 else through
            for part in range(2):
                tile_image[tile, pl.ds(number, 1), pl.ds(part * LANES, LANES)] = jnp.where(
                    upper_row, quad[2 * part + 1 : 2 * part + 2], quad[2 * part : 2 * part + 1]
                )

    for copy in tiles:
        copy.wait_send()


def store_kernel(final, tile_image, final_out, image_out, sems):
    copies = [
        pltpu.make_async_copy(final.at[index], final_out.at[index], sems.at[index]) for index in range(POPS)
    ]
    copies.append(pltpu.make_async_copy(tile_image, image_out, sems.at[POPS]))
    for copy in copies:
        copy.start()
    for copy in copies:
        copy.wait()


def on_device(populations, camera, active_list, tile_order):
    spans = lax.axis_size("span")
    streams = lax.axis_size("stream")
    vmem = functools.partial(pl.BlockSpec, memory_space=pltpu.VMEM)
    pinned = functools.partial(pltpu.with_memory_space_constraint, memory_space=pltpu.HBM)
    anywhere = functools.partial(pl.BlockSpec, memory_space=pl.ANY)
    post = pltpu.VMEM((POPS, PLACES, ROWS, LANES), jnp.float32)
    final, tile_image = pl.pallas_call(
        functools.partial(kernel, spans, streams),
        out_shape=(
            jax.ShapeDtypeStruct(populations.shape, jnp.float32),
            jax.ShapeDtypeStruct((2, 4, 256), jnp.float32),
        ),
        in_specs=[anywhere()] * 4,
        out_specs=(vmem(), vmem()),
        scratch_shapes=[
            pltpu.SMEM(camera.shape, jnp.int32),
            pltpu.SMEM((active_list.size,), jnp.int32),
            pltpu.SMEM((tile_order.size,), jnp.int32),
            pltpu.VMEM((POPS, COLUMNS, PLANES, LANES), jnp.float32),
            post,
            post,
            post,
            pltpu.VMEM((3, PLACES, ROWS, LANES), jnp.float32),
            pltpu.VMEM((2, 2, 5, COLUMNS, LANES), jnp.float32),
            pltpu.VMEM((2, POPS, COLUMNS, LANES), jnp.float32),
            pltpu.VMEM((2, 5, COLUMNS, LANES), jnp.float32),
            pltpu.VMEM((3, 2, 3, PLANES, LANES), jnp.float32),
            pltpu.VMEM((3, 2, 3, PLANES, LANES), jnp.float32),
            pltpu.VMEM((3, PLANES, LANES), jnp.float32),
            pltpu.VMEM((8, 16, LANES), jnp.float32),
            pltpu.VMEM((8, 16, LANES), jnp.float32),
            pltpu.VMEM((spans, 2, 16, LANES), jnp.float32),
            pltpu.SemaphoreType.DMA((MESSAGES,)),
            pltpu.SemaphoreType.DMA((MESSAGES,)),
            pltpu.SemaphoreType.DMA((COLUMNS,)),
            pltpu.SemaphoreType.DMA,
            pltpu.SemaphoreType.DMA((3,)),
        ],
        compiler_params=pltpu.CompilerParams(
            collective_id=0, has_side_effects=True, vmem_limit_bytes=48 * 1024 * 1024
        ),
    )(populations, camera, pinned(active_list.reshape(-1)), pinned(tile_order.reshape(-1)))
    return pl.pallas_call(
        store_kernel,
        out_shape=(
            jax.ShapeDtypeStruct(final.shape, jnp.float32),
            jax.ShapeDtypeStruct(tile_image.shape, jnp.float32),
        ),
        in_specs=[anywhere()] * 2,
        out_specs=(anywhere(), anywhere()),
        scratch_shapes=[pltpu.SemaphoreType.DMA((POPS + 1,))],
        compiler_params=pltpu.CompilerParams(vmem_limit_bytes=1024 * 1024),
    )(final, tile_image)


def solution(mesh):
    placed = (P(None, "stream", "span"), P("stream"), P("stream", "span", None), P("stream", None))
    return jax.shard_map(
        on_device,
        mesh=mesh,
        in_specs=placed,
        out_specs=(P(None, "stream", "span"), P(("stream", "span"), None, None)),
        check_vma=False,
    )
```

```python
import functools
import math

import jax
import jax.numpy as jnp
from jax import lax
from jax.experimental import pallas as pl
from jax.experimental.pallas import tpu as pltpu
from jax.sharding import PartitionSpec as P

MESH = pl.DeviceIdType.MESH

NZ = 64
LANES = 128
POPS = 19
PLANES = 32
COLUMNS = 16
TOP = 8
ROWS = 48
BLOCKS = PLANES // 8

VELOCITIES = (
    (0, 0, 0),
    (1, 0, 0),
    (-1, 0, 0),
    (0, 1, 0),
    (0, -1, 0),
    (0, 0, 1),
    (0, 0, -1),
    (1, 1, 0),
    (-1, -1, 0),
    (1, -1, 0),
    (-1, 1, 0),
    (1, 0, 1),
    (-1, 0, -1),
    (1, 0, -1),
    (-1, 0, 1),
    (0, 1, 1),
    (0, -1, -1),
    (0, 1, -1),
    (0, -1, 1),
)
OPPOSITE = (0, 2, 1, 4, 3, 6, 5, 8, 7, 10, 9, 12, 11, 14, 13, 16, 15, 18, 17)
TAU_ZERO = 0.55
SMAGORINSKY = 0.17
VORTEX_SCALE = 0.003
SPEED_SCALE = 0.08
OPACITY_GAIN = 0.03

ORDER = (1, 9, 7, 11, 13, 3, 15, 17, 0, 5, 6, 4, 16, 18, 12, 14, 10, 2, 8)
SLOT = tuple(ORDER.index(index) for index in range(POPS))
X_UP, LATE_UP = (0, 5), (5, 11)
X_DOWN, LATE_DOWN = (14, 5), (3, 11)
Y_PACKS = (((7, 3), (15, 17)), ((8, 4), (16, 18)))
Y_ALONE = (10, 9)
RIM_ROWS = 2 * PLANES + PLANES // 2
SPEED_ROWS = PLANES + PLANES // 2

PLACES = COLUMNS + 2
POST_MESSAGES = 8
SPEED_BASE = 3 * POST_MESSAGES
LATE_BASE = SPEED_BASE + 2
TILE_BASE = LATE_BASE + 12
MESSAGES = TILE_BASE + 3


def reciprocal(value):
    return pl.reciprocal(value, approx=True)


def moments(f):
    pair = {index: f[index] + f[index + 1] for index in range(1, POPS, 2)}
    gap = {index: f[index] - f[index + 1] for index in range(1, POPS, 2)}
    flow = (
        (gap[1] + gap[7]) + (gap[9] + gap[11]) + gap[13],
        (gap[3] + gap[7]) + (gap[15] - gap[9]) + gap[17],
        (gap[5] + gap[11]) + (gap[15] - gap[13]) - gap[17],
    )
    around_xy = pair[7] + pair[9]
    around_xz = pair[11] + pair[13]
    around_yz = pair[15] + pair[17]
    along_x = pair[1] + (around_xy + around_xz)
    density = (f[0] + pair[3]) + (pair[5] + around_yz) + along_x
    return pair, flow, (around_xy, around_xz, around_yz), along_x, density


def collide(f):
    pair, flow, around, along_x, density = moments(f)
    along_y = pair[3] + (around[0] + around[2])
    along_z = pair[5] + (around[1] + around[2])
    inverse = reciprocal(density)
    triple = 3.0 * inverse
    ninth = 9.0 * inverse
    vx, vy, vz = [part * triple for part in flow]
    vxx, vyy, vzz = vx * vx, vy * vy, vz * vz
    vxy, vxz, vyz = vx * vy, vx * vz, vy * vz
    qxx = ninth * along_x - (3.0 + vxx)
    qyy = ninth * along_y - (3.0 + vyy)
    qzz = ninth * along_z - (3.0 + vzz)
    qxy = ninth * (pair[7] - pair[9]) - vxy
    qxz = ninth * (pair[11] - pair[13]) - vxz
    qyz = ninth * (pair[15] - pair[17]) - vyz
    cross = qxy * qxy + qxz * qxz + qyz * qyz
    square = (qxx * qxx + qyy * qyy) + (qzz * qzz + (cross + cross))
    magnitude = square * lax.rsqrt(jnp.maximum(square, 1e-30))
    inner = TAU_ZERO * TAU_ZERO + (18.0 * math.sqrt(2.0) * SMAGORINSKY * SMAGORINSKY / 9.0) * magnitude
    rate = 2.0 * reciprocal(TAU_ZERO + inner * lax.rsqrt(inner))
    keep = 1.0 - rate
    weight = (rate * density) * (1.0 / 36.0)
    bx, by, bz = weight * vx, weight * vy, weight * vz
    half = 0.5 * weight
    ax, ay, az = half * vxx, half * vyy, half * vzz
    base = weight - (ax + ay + az) * (1.0 / 3.0)
    ex, ey, ez = base + ax, base + ay, base + az
    out = [None] * POPS
    out[0] = keep * f[0] + 12.0 * base
    for index, even, odd in ((1, ex, bx), (3, ey, by), (5, ez, bz)):
        out[index] = keep * f[index] + 2.0 * (even + odd)
        out[index + 1] = keep * f[index + 1] + 2.0 * (even - odd)
    for index, first, second, middle, mixed in (
        (7, bx, by, ex + ay, weight * vxy),
        (11, bx, bz, ex + az, weight * vxz),
        (15, by, bz, ey + az, weight * vyz),
    ):
        same, other = middle + mixed, middle - mixed
        plus, minus = first + second, first - second
        out[index] = keep * f[index] + (same + plus)
        out[index + 1] = keep * f[index + 1] + (same - plus)
        out[index + 2] = keep * f[index + 2] + (other + minus)
        out[index + 3] = keep * f[index + 3] + (other - minus)
    return out


def kernel(
    spans,
    streams,
    populations,
    camera_in,
    active_in,
    order_in,
    final,
    tile_image,
    camera,
    active_list,
    tile_order,
    field,
    post0,
    post1,
    post2,
    speed,
    strips,
    deep,
    second,
    rims,
    arrived,
    speed_rims,
    speed_arrived,
    shaded,
    foot,
    outgoing,
    incoming,
    send_sem,
    recv_sem,
    load_sem,
    own_sem,
    small_sem,
):
    stream = lax.axis_index("stream")
    span = lax.axis_index("span")
    stream_up = lax.rem(stream + 1, streams)
    stream_down = lax.rem(stream + streams - 1, streams)
    span_up = lax.rem(span + 1, spans)
    span_down = lax.rem(span + spans - 1, spans)
    span_far = lax.rem(span + 2, spans)

    barrier = pltpu.get_barrier_semaphore()
    partners = (
        (stream_up, span),
        (stream_down, span),
        (stream, span_up),
        (stream, span_down),
        (stream_up, span_up),
        (stream_up, span_down),
        (stream_down, span_up),
        (stream_down, span_down),
        (stream, span_far),
    )
    for partner in partners:
        pl.semaphore_signal(barrier, inc=1, device_id=partner, device_id_type=MESH)

    loads = [None] * COLUMNS
    for k in range(COLUMNS // 2):
        for column in (k, COLUMNS - 1 - k):
            loads[column] = pltpu.make_async_copy(
                populations.at[:, :, pl.ds(column * LANES, LANES)], field.at[:, column], load_sem.at[column]
            )
            loads[column].start()
    small = [
        pltpu.make_async_copy(source, target, small_sem.at[number])
        for number, (source, target) in enumerate(
            ((camera_in, camera), (active_in, active_list), (order_in, tile_order))
        )
    ]
    for copy in small:
        copy.start()

    lane = lax.broadcasted_iota(jnp.int32, (8, LANES), 1)
    upper = lane >= NZ
    level = lax.rem(lane, NZ)
    floor = level == 0
    ceiling = level == NZ - 1

    def remote(source, target, number, device):
        return pltpu.make_async_remote_copy(
            src_ref=source,
            dst_ref=target,
            send_sem=send_sem.at[number],
            recv_sem=recv_sem.at[number],
            device_id=device,
            device_id_type=MESH,
        )

    before_row, after_row = TOP - 1, TOP + PLANES
    before_place, after_place = 0, PLACES - 1

    def x_copies(buffer, up_strip, down_strip, up, down, depth, number):
        places = pl.ds(1, COLUMNS)
        return [
            remote(up_strip, buffer.at[pl.ds(*up), places, before_row - depth], number, (stream_up, span)),
            remote(down_strip, buffer.at[pl.ds(*down), places, after_row + depth], number + 1, (stream_down, span)),
        ]

    def y_copies(up_source, up_target, down_source, down_target, number):
        return [
            remote(up_source, up_target, number, (stream, span_up)),
            remote(down_source, down_target, number + 1, (stream, span_down)),
        ]

    corner_paths = (
        (7, 0, COLUMNS - 1, before_place, before_row, (stream_up, span_up)),
        (9, 0, 0, after_place, before_row, (stream_up, span_down)),
        (10, 1, COLUMNS - 1, before_place, after_row, (stream_down, span_up)),
        (8, 1, 0, after_place, after_row, (stream_down, span_down)),
    )

    def corner_copies(buffer, strip, number, first, count=1, depth=0):
        copies = []
        for index, side, column, place, row, device in corner_paths:
            slot = SLOT[index] if count == 1 else SLOT[3 if column else 4]
            outwards = -depth if row == before_row else depth
            copies.append(
                remote(
                    strip[side].at[pl.ds(slot - first[side], count), pl.ds(column, 1)],
                    buffer.at[pl.ds(slot, count), place, pl.ds(row + outwards, 1)],
                    number + len(copies),
                    device,
                )
            )
        return copies

    def joined(along_y, before, here, after):
        if along_y == 1:
            return jnp.where(upper, before(), here())
        if along_y == -1:
            return jnp.where(upper, here(), after())
        return here()

    def block_reader(buffer, place, block):
        def read(slot, along_y, plane):
            rows = pl.ds(TOP + 8 * block + plane, 8)
            return joined(
                along_y,
                lambda: buffer[slot, place - 1, rows],
                lambda: buffer[slot, place, rows],
                lambda: buffer[slot, place + 1, rows],
            )

        return read

    def strip_reader(buffer, plane, column):
        flat = buffer.reshape(buffer.shape[0], PLACES * ROWS, LANES)
        first = (column + 1) * ROWS + TOP + plane

        def read(slot, along_y, along):
            def at(step):
                return lambda: flat[slot, pl.ds(first + step * ROWS + along, 8, stride=ROWS)]

            return joined(along_y, at(-1), at(0), at(1))

        return read

    def rim_reader(buffer, block):
        def read(slot, along_y, plane):
            rows = pl.ds(TOP + 8 * block + plane, 8)
            high, low = {0: (COLUMNS, 1), 1: (0, COLUMNS), -1: (1, PLACES - 1)}[along_y]
            return jnp.where(upper, buffer[slot, high, rows], buffer[slot, low, rows])

        return read

    def streamed(read):
        values = []
        for index in range(POPS):
            along_x, along_y, along_z = VELOCITIES[index]
            value = read(SLOT[index], along_y, -along_x)
            shift = ((NZ if along_y else 0) + along_z) % LANES
            if shift:
                value = pltpu.roll(value, shift, 1)
            if along_z:
                value = jnp.where(
                    floor if along_z > 0 else ceiling, read(SLOT[OPPOSITE[index]], 0, 0), value
                )
            values.append(value)
        return values

    def sweep(work, first, last, step, blocks, start=0, stop=None):
        def body(k, carry):
            for part in range(step):
                work(first + step * k + part, blocks)
            return carry

        lax.fori_loop(start, (last - first) // step if stop is None else stop, body, 0)

    everything = tuple(range(BLOCKS))

    def inner(work, start=0, stop=None):
        sweep(work, 1, COLUMNS - 1, 7, (1, 2), start, stop)

    def outer(work):
        for column in (0, COLUMNS - 1):
            work(column, (1, 2))
        sweep(work, 0, COLUMNS, 8, (0, 3))

    sent = []

    def send(copies):
        for copy in copies:
            copy.start()
        sent.extend(copies)

    buffers = (post0, post1, post2)
    edge_strips = [(strips.at[phase, 0], strips.at[phase, 1]) for phase in range(2)]
    edge_strips.append((deep.at[0, pl.ds(*X_UP)], deep.at[1, pl.ds(*X_DOWN)]))
    x_sides, corners = [], []
    for phase, buffer in enumerate(buffers):
        number = phase * POST_MESSAGES
        x_sides.append(x_copies(buffer, *edge_strips[phase], X_UP, X_DOWN, 0, number))
        if phase < 2:
            corners.append(
                corner_copies(buffer, edge_strips[phase], number + 2, (X_UP[0], X_DOWN[0]))
            )
        else:
            corners.append(corner_copies(buffer, (deep.at[0], deep.at[1]), number + 2, (0, 0)))
    late = x_copies(
        post2, deep.at[0, pl.ds(*LATE_UP)], deep.at[1, pl.ds(*LATE_DOWN)], LATE_UP, LATE_DOWN, 0, LATE_BASE
    )
    late += x_copies(post2, second.at[0], second.at[1], X_UP, X_DOWN, 1, LATE_BASE + 2)
    late += corner_copies(post2, (deep.at[0], deep.at[1]), LATE_BASE + 4, (0, 0), count=3)
    late += corner_copies(
        post2, (second.at[0], second.at[1]), LATE_BASE + 8, (X_UP[0], X_DOWN[0]), depth=1
    )
    y_sides = [
        y_copies(
            rims.at[phase, 0],
            arrived.at[phase, 0],
            rims.at[phase, 1],
            arrived.at[phase, 1],
            phase * POST_MESSAGES + 6,
        )
        for phase in range(3)
    ]

    def post_strips(values_of, planes, store):
        for side in range(2):
            for half in range(2):
                out = collide(values_of(planes[side], 8 * half))
                store(side, pl.ds(8 * half, 8), out)

    def store_edges(phase):
        def store(side, rows, out):
            first, count = (X_UP, X_DOWN)[side]
            for place in range(count):
                strips[phase, side, place, rows] = out[ORDER[first + place]]

        return store

    def store_deep(side, rows, out):
        for index in range(POPS):
            deep[side, SLOT[index], rows] = out[index]

    def store_second(side, rows, out):
        first, count = (X_UP, X_DOWN)[side]
        for place in range(count):
            second[side, place, rows] = out[ORDER[first + place]]

    edge_planes, second_planes = (PLANES - 1, 0), (PLANES - 2, 1)

    def packed(side, own, other):
        turned = pltpu.roll(other, NZ, 1)
        return jnp.where(upper, turned, own) if side else jnp.where(upper, own, turned)

    def post_rims(phase, values_of):
        alone = []
        for block in range(BLOCKS):
            out = collide(values_of(block))
            for side in range(2):
                for pack, (first, second) in enumerate(Y_PACKS[side]):
                    rims[phase, side, pl.ds(pack * PLANES + 8 * block, 8)] = packed(side, out[first], out[second])
            alone.append([out[index] for index in Y_ALONE])
        for block in range(BLOCKS // 2):
            for side in range(2):
                rims[phase, side, pl.ds(2 * PLANES + 8 * block, 8)] = packed(
                    side, alone[block][side], alone[block + BLOCKS // 2][side]
                )

    def await_rims(phase):
        for copy in x_sides[phase] + corners[phase] + y_sides[phase]:
            copy.wait_recv()
        buffer = buffers[phase]
        for side, place in enumerate((before_place, after_place)):
            for block in range(BLOCKS):
                rows = pl.ds(TOP + 8 * block, 8)
                for pack, (first, second) in enumerate(Y_PACKS[side]):
                    value = arrived[phase, side, pl.ds(pack * PLANES + 8 * block, 8)]
                    buffer[SLOT[first], place, rows] = value
                    buffer[SLOT[second], place, rows] = pltpu.roll(value, NZ, 1)
            for block in range(BLOCKS // 2):
                value = arrived[phase, side, pl.ds(2 * PLANES + 8 * block, 8)]
                slot = SLOT[Y_ALONE[side]]
                buffer[slot, place, pl.ds(TOP + 8 * block, 8)] = value
                buffer[slot, place, pl.ds(TOP + PLANES // 2 + 8 * block, 8)] = pltpu.roll(value, NZ, 1)

    def post_column(target, column, blocks, values_of):
        for block in blocks:
            out = collide(values_of(block))
            for index in range(POPS):
                target[SLOT[index], column + 1, pl.ds(TOP + 8 * block, 8)] = out[index]

    def first_work(column, blocks):
        post_column(
            post0,
            column,
            blocks,
            lambda block: [field[index, column, pl.ds(8 * block, 8)] for index in range(POPS)],
        )

    for column in (0, COLUMNS - 1):
        loads[column].wait()
    post_rims(
        0,
        lambda block: [
            jnp.where(upper, field[index, COLUMNS - 1, pl.ds(8 * block, 8)], field[index, 0, pl.ds(8 * block, 8)])
            for index in range(POPS)
        ],
    )
    for column in range(1, COLUMNS - 1):
        loads[column].wait()
    flat_field = field.reshape(POPS, COLUMNS * PLANES, LANES)
    post_strips(
        lambda plane, column: [
            flat_field[index, pl.ds(column * PLANES + plane, 8, stride=PLANES)] for index in range(POPS)
        ],
        edge_planes,
        store_edges(0),
    )
    seam = (stream == 0).astype(jnp.int32)
    sweep(first_work, 0, COLUMNS, 4, everything, 0, 4 * seam)
    pl.semaphore_wait(barrier, len(partners))
    send(x_sides[0] + corners[0] + y_sides[0])
    sweep(first_work, 0, COLUMNS, 4, everything, 4 * seam)

    for phase in (1, 2):
        source, target = buffers[phase - 1], buffers[phase]

        def step_work(column, blocks):
            post_column(target, column, blocks, lambda block: streamed(block_reader(source, column + 1, block)))

        def strip_values(plane, column):
            return streamed(strip_reader(source, plane, column))

        inner(step_work)
        await_rims(phase - 1)
        post_strips(strip_values, edge_planes, store_edges(phase) if phase == 1 else store_deep)
        send(x_sides[phase] + corners[phase])
        if phase == 2:
            post_strips(strip_values, second_planes, store_second)
            send(late)
        post_rims(phase, lambda block: streamed(rim_reader(source, block)))
        send(y_sides[phase])
        outer(step_work)

    def velocity(values):
        _, flow, _, _, density = moments(values)
        inverse = reciprocal(density)
        return [part * inverse for part in flow]

    def last_work(column, blocks):
        lanes = pl.ds(pl.multiple_of(column * LANES, LANES), LANES)
        for block in blocks:
            values = streamed(block_reader(post2, column + 1, block))
            for index in range(POPS):
                final[index, pl.ds(8 * block, 8), lanes] = values[index]
            for dimension, part in enumerate(velocity(values)):
                speed[dimension, column + 1, pl.ds(TOP + 8 * block, 8)] = part

    inner(last_work)
    await_rims(2)
    parts = [velocity(streamed(rim_reader(post2, block))) for block in range(BLOCKS)]
    for side in range(2):
        for block in range(BLOCKS):
            speed_rims[side, pl.ds(8 * block, 8)] = packed(side, parts[block][0], parts[block][1])
        for block in range(BLOCKS // 2):
            speed_rims[side, pl.ds(PLANES + 8 * block, 8)] = packed(
                side, parts[block][2], parts[block + BLOCKS // 2][2]
            )
    speed_y = y_copies(
        speed_rims.at[0], speed_arrived.at[0], speed_rims.at[1], speed_arrived.at[1], SPEED_BASE
    )
    send(speed_y)
    outer(last_work)

    for copy in small:
        copy.wait()

    bits = jnp.int32(0)
    for entry in range(32):
        number = active_list[entry]
        bits = bits | jnp.where(number < 32, jnp.left_shift(jnp.int32(1), jnp.minimum(number, 31)), 0)
    falling = jnp.full((8, LANES), camera[0], jnp.int32) == 1
    leading = falling == upper
    bits = jnp.full((8, LANES), bits, jnp.int32)
    corner = 4 * (lax.broadcasted_iota(jnp.int32, (8, LANES), 0) // 4)

    def shade_with(read, brick, store):
        centre = [read(dimension, 0, 0) for dimension in range(3)]
        slope_x, slope_y, slope_z = [], [], []
        for dimension in range(3):
            here = centre[dimension]
            slope_x.append(read(dimension, 0, 1) - read(dimension, 0, -1))
            slope_y.append(pltpu.roll(read(dimension, -1, 0) - read(dimension, 1, 0), NZ, 1))
            above = jnp.where(ceiling, -here, pltpu.roll(here, LANES - 1, 1))
            below = jnp.where(floor, -here, pltpu.roll(here, 1, 1))
            slope_z.append(above - below)
        cross = slope_x[1] * slope_y[0] + slope_x[2] * slope_z[0] + slope_y[2] * slope_z[1]
        total = slope_x[0] * slope_x[0] + slope_y[1] * slope_y[1] + slope_z[2] * slope_z[2] + (cross + cross)
        vortex = total * (-0.125 / VORTEX_SCALE)
        small = jnp.exp(-jnp.abs(vortex))
        one = 1.0 + small
        share = reciprocal(one)
        colours = [jnp.where(vortex >= 0.0, share, small * share)]
        for dimension in (0, 2):
            colours.append(reciprocal(1.0 + jnp.exp(centre[dimension] * (-1.0 / SPEED_SCALE))))
        passing = jnp.exp(-OPACITY_GAIN * (jnp.maximum(vortex, 0.0) + jnp.log(one)))
        passing = jnp.where((jnp.right_shift(bits, brick) & 1) == 1, passing, 1.0)
        other = pltpu.roll(passing, NZ, 1)
        weight = (1.0 - passing) * jnp.where(leading, 1.0, other)
        for number in range(3):
            store(number, colours[number] * weight)
        store(3, passing * other)

    def shade(column, blocks):
        for block in blocks:

            def store(number, value):
                shaded[number, column, pl.ds(8 * block, 8)] = value

            shade_with(block_reader(speed, column + 1, block), corner + (8 * block + column // 4), store)

    flat_shaded = shaded.reshape(4, COLUMNS * PLANES, LANES)

    def shade_strip(plane, first):
        def store(number, value):
            flat_shaded[number, pl.ds(first * PLANES + plane, 8, stride=PLANES)] = value

        brick = (lax.broadcasted_iota(jnp.int32, (8, LANES), 0) + first) // 4
        shade_with(strip_reader(speed, plane, first), brick + plane // 4 * 4, store)

    for plane in (-1, PLANES):
        for place in range(1, COLUMNS + 1):
            speed[:, place, pl.ds(TOP + plane, 1)] = jnp.zeros((3, 1, LANES), jnp.float32)
    sweep(shade, 1, COLUMNS - 1, 7, (1, 2))
    sweep(shade, 1, COLUMNS - 1, 7, (0, 3))
    for copy in late:
        copy.wait_recv()
    flat_speed = speed.reshape(3, PLACES * ROWS, LANES)
    for plane in (-1, PLANES):
        for first in (0, 8):
            for dimension, part in enumerate(velocity(streamed(strip_reader(post2, plane, first)))):
                flat_speed[dimension, pl.ds((first + 1) * ROWS + TOP + plane, 8, stride=ROWS)] = part
    for plane in (0, PLANES - 1):
        for first in (1, 7):
            shade_strip(plane, first)

    def walk(side, block, first, last, state):
        from_back = falling if side == 1 else jnp.logical_not(falling)
        colours, through = state[:3], state[3]
        for k in range(first, last, -1):
            column = k if side == 0 else COLUMNS - 1 - k
            pair = [shaded[number, column, pl.ds(8 * block, 8)] for number in range(4)]
            fade = jnp.where(from_back, pair[3], 1.0)
            veil = jnp.where(from_back, 1.0, through)
            colours = [colours[number] * fade + pair[number] * veil for number in range(3)]
            through = through * pair[3]
        return colours + [through]

    sums = {}
    for block in range(BLOCKS):
        for side in range(2):
            start = [jnp.zeros((8, LANES), jnp.float32)] * 3 + [jnp.ones((8, LANES), jnp.float32)]
            sums[side, block] = walk(side, block, COLUMNS // 2 - 1, 0, start)
    for copy in speed_y:
        copy.wait_recv()
    for side, place in enumerate((before_place, after_place)):
        for block in range(BLOCKS):
            value = speed_arrived[side, pl.ds(8 * block, 8)]
            rows = pl.ds(TOP + 8 * block, 8)
            speed[0, place, rows] = value
            speed[1, place, rows] = pltpu.roll(value, NZ, 1)
        for block in range(BLOCKS // 2):
            value = speed_arrived[side, pl.ds(PLANES + 8 * block, 8)]
            speed[2, place, pl.ds(TOP + 8 * block, 8)] = value
            speed[2, place, pl.ds(TOP + PLANES // 2 + 8 * block, 8)] = pltpu.roll(value, NZ, 1)
    for column in (0, COLUMNS - 1):
        shade(column, everything)
    for side, block in sums:
        sums[side, block] = walk(side, block, 0, -1, sums[side, block])

    for block in range(BLOCKS):
        low, high = sums[0, block], sums[1, block]
        front = [jnp.where(falling, b, a) for a, b in zip(low, high)]
        back = [jnp.where(falling, a, b) for a, b in zip(low, high)]
        for number in range(4):
            if number < 3:
                half = front[number] + front[3] * back[number]
                value = half + pltpu.roll(half, NZ, 1)
            else:
                value = front[3] * back[3]
            for part in range(2):
                foot[2 * block + part, pl.ds(4 * number, 4)] = value[4 * part : 4 * part + 4]

    for number in range(8):
        outgoing[number] = foot[tile_order[number]]
    tiles = []
    for hop, target in enumerate((span_up, span_down, span_far)):
        tiles.append(
            remote(
                outgoing.at[pl.ds(2 * target, 2)], incoming.at[span], TILE_BASE + hop, (stream, target)
            )
        )
    earlier = list(sent)
    send(tiles)
    own = pltpu.make_async_copy(outgoing.at[pl.ds(2 * span, 2)], incoming.at[span], own_sem)
    own.start()
    own.wait()
    for copy in earlier:
        copy.wait_send()
    for copy in tiles:
        copy.wait_recv()
    wide = jnp.broadcast_to(camera[0], (16, LANES)) == 1
    upper_row = lax.broadcasted_iota(jnp.int32, (1, LANES), 1) >= NZ
    for tile in range(2):
        sheets = [incoming[source, tile] for source in range(spans)]
        colour = sheets[0][:12]
        through = sheets[0][12:]
        for source in range(1, spans):
            sheet = sheets[source]
            fade = jnp.concatenate([sheet[12:]] * 3, axis=0)
            veil = jnp.concatenate([through] * 3, axis=0)
            colour = jnp.where(wide[:12], colour * fade + sheet[:12], colour + veil * sheet[:12])
            through = through * sheet[12:]
        for number in range(4):
            quad = colour[4 * number : 4 * number + 4] if number < 3 else through
            for part in range(2):
                tile_image[tile, pl.ds(number, 1), pl.ds(part * LANES, LANES)] = jnp.where(
                    upper_row, quad[2 * part + 1 : 2 * part + 2], quad[2 * part : 2 * part + 1]
                )

    for copy in tiles:
        copy.wait_send()


def store_kernel(final, tile_image, final_out, image_out, sems):
    copies = [
        pltpu.make_async_copy(final.at[index], final_out.at[index], sems.at[index]) for index in range(POPS)
    ]
    copies.append(pltpu.make_async_copy(tile_image, image_out, sems.at[POPS]))
    for copy in copies:
        copy.start()
    for copy in copies:
        copy.wait()


def on_device(populations, camera, active_list, tile_order):
    spans = lax.axis_size("span")
    streams = lax.axis_size("stream")
    vmem = functools.partial(pl.BlockSpec, memory_space=pltpu.VMEM)
    pinned = functools.partial(pltpu.with_memory_space_constraint, memory_space=pltpu.HBM)
    anywhere = functools.partial(pl.BlockSpec, memory_space=pl.ANY)
    post = pltpu.VMEM((POPS, PLACES, ROWS, LANES), jnp.float32)
    final, tile_image = pl.pallas_call(
        functools.partial(kernel, spans, streams),
        out_shape=(
            jax.ShapeDtypeStruct(populations.shape, jnp.float32),
            jax.ShapeDtypeStruct((2, 4, 256), jnp.float32),
        ),
        in_specs=[anywhere()] * 4,
        out_specs=(vmem(), vmem()),
        scratch_shapes=[
            pltpu.SMEM(camera.shape, jnp.int32),
            pltpu.SMEM((active_list.size,), jnp.int32),
            pltpu.SMEM((tile_order.size,), jnp.int32),
            pltpu.VMEM((POPS, COLUMNS, PLANES, LANES), jnp.float32),
            post,
            post,
            post,
            pltpu.VMEM((3, PLACES, ROWS, LANES), jnp.float32),
            pltpu.VMEM((2, 2, 5, COLUMNS, LANES), jnp.float32),
            pltpu.VMEM((2, POPS, COLUMNS, LANES), jnp.float32),
            pltpu.VMEM((2, 5, COLUMNS, LANES), jnp.float32),
            pltpu.VMEM((3, 2, RIM_ROWS, LANES), jnp.float32),
            pltpu.VMEM((3, 2, RIM_ROWS, LANES), jnp.float32),
            pltpu.VMEM((2, SPEED_ROWS, LANES), jnp.float32),
            pltpu.VMEM((2, SPEED_ROWS, LANES), jnp.float32),
            pltpu.VMEM((4, COLUMNS, PLANES, LANES), jnp.float32),
            pltpu.VMEM((8, 16, LANES), jnp.float32),
            pltpu.VMEM((8, 16, LANES), jnp.float32),
            pltpu.VMEM((spans, 2, 16, LANES), jnp.float32),
            pltpu.SemaphoreType.DMA((MESSAGES,)),
            pltpu.SemaphoreType.DMA((MESSAGES,)),
            pltpu.SemaphoreType.DMA((COLUMNS,)),
            pltpu.SemaphoreType.DMA,
            pltpu.SemaphoreType.DMA((3,)),
        ],
        compiler_params=pltpu.CompilerParams(
            collective_id=0, has_side_effects=True, vmem_limit_bytes=48 * 1024 * 1024
        ),
    )(populations, camera, pinned(active_list.reshape(-1)), pinned(tile_order.reshape(-1)))
    return pl.pallas_call(
        store_kernel,
        out_shape=(
            jax.ShapeDtypeStruct(final.shape, jnp.float32),
            jax.ShapeDtypeStruct(tile_image.shape, jnp.float32),
        ),
        in_specs=[anywhere()] * 2,
        out_specs=(anywhere(), anywhere()),
        scratch_shapes=[pltpu.SemaphoreType.DMA((POPS + 1,))],
        compiler_params=pltpu.CompilerParams(vmem_limit_bytes=1024 * 1024),
    )(final, tile_image)


def solution(mesh):
    placed = (P(None, "stream", "span"), P("stream"), P("stream", "span", None), P("stream", None))
    return jax.shard_map(
        on_device,
        mesh=mesh,
        in_specs=placed,
        out_specs=(P(None, "stream", "span"), P(("stream", "span"), None, None)),
        check_vma=False,
    )
```

```python
import functools
import math

import jax
import jax.numpy as jnp
from jax import lax
from jax.experimental import pallas as pl
from jax.experimental.pallas import tpu as pltpu
from jax.sharding import PartitionSpec as P

MESH = pl.DeviceIdType.MESH

NZ = 64
LANES = 128
POPS = 19
PLANES = 32
COLUMNS = 16
TOP = 8
ROWS = 48
BLOCKS = PLANES // 8

VELOCITIES = (
    (0, 0, 0),
    (1, 0, 0),
    (-1, 0, 0),
    (0, 1, 0),
    (0, -1, 0),
    (0, 0, 1),
    (0, 0, -1),
    (1, 1, 0),
    (-1, -1, 0),
    (1, -1, 0),
    (-1, 1, 0),
    (1, 0, 1),
    (-1, 0, -1),
    (1, 0, -1),
    (-1, 0, 1),
    (0, 1, 1),
    (0, -1, -1),
    (0, 1, -1),
    (0, -1, 1),
)
OPPOSITE = (0, 2, 1, 4, 3, 6, 5, 8, 7, 10, 9, 12, 11, 14, 13, 16, 15, 18, 17)
TAU_ZERO = 0.55
SMAGORINSKY = 0.17
VORTEX_SCALE = 0.003
SPEED_SCALE = 0.08
OPACITY_GAIN = 0.03

ORDER = (1, 9, 7, 11, 13, 3, 15, 17, 0, 5, 6, 4, 16, 18, 12, 14, 10, 2, 8)
SLOT = tuple(ORDER.index(index) for index in range(POPS))
X_UP, LATE_UP = (0, 5), (5, 11)
X_DOWN, LATE_DOWN = (14, 5), (3, 11)
Y_PACKS = (((7, 3), (15, 17)), ((8, 4), (16, 18)))
Y_ALONE = (10, 9)
RIM_ROWS = 2 * PLANES + PLANES // 2
SPEED_ROWS = PLANES + PLANES // 2

PLACES = COLUMNS + 2
POST_MESSAGES = 8
SPEED_BASE = 3 * POST_MESSAGES
LATE_BASE = SPEED_BASE + 2
TILE_BASE = LATE_BASE + 12
MESSAGES = TILE_BASE + 3


def reciprocal(value):
    return pl.reciprocal(value, approx=True)


def moments(f):
    pair = {index: f[index] + f[index + 1] for index in range(1, POPS, 2)}
    gap = {index: f[index] - f[index + 1] for index in range(1, POPS, 2)}
    flow = (
        (gap[1] + gap[7]) + (gap[9] + gap[11]) + gap[13],
        (gap[3] + gap[7]) + (gap[15] - gap[9]) + gap[17],
        (gap[5] + gap[11]) + (gap[15] - gap[13]) - gap[17],
    )
    around_xy = pair[7] + pair[9]
    around_xz = pair[11] + pair[13]
    around_yz = pair[15] + pair[17]
    along_x = pair[1] + (around_xy + around_xz)
    density = (f[0] + pair[3]) + (pair[5] + around_yz) + along_x
    return pair, flow, (around_xy, around_xz, around_yz), along_x, density


def collide(f):
    pair, flow, around, along_x, density = moments(f)
    along_y = pair[3] + (around[0] + around[2])
    along_z = pair[5] + (around[1] + around[2])
    inverse = reciprocal(density)
    triple = 3.0 * inverse
    ninth = 9.0 * inverse
    vx, vy, vz = [part * triple for part in flow]
    vxx, vyy, vzz = vx * vx, vy * vy, vz * vz
    vxy, vxz, vyz = vx * vy, vx * vz, vy * vz
    qxx = ninth * along_x - (3.0 + vxx)
    qyy = ninth * along_y - (3.0 + vyy)
    qzz = ninth * along_z - (3.0 + vzz)
    qxy = ninth * (pair[7] - pair[9]) - vxy
    qxz = ninth * (pair[11] - pair[13]) - vxz
    qyz = ninth * (pair[15] - pair[17]) - vyz
    cross = qxy * qxy + qxz * qxz + qyz * qyz
    square = (qxx * qxx + qyy * qyy) + (qzz * qzz + (cross + cross))
    magnitude = square * lax.rsqrt(jnp.maximum(square, 1e-30))
    inner = TAU_ZERO * TAU_ZERO + (18.0 * math.sqrt(2.0) * SMAGORINSKY * SMAGORINSKY / 9.0) * magnitude
    rate = 2.0 * reciprocal(TAU_ZERO + inner * lax.rsqrt(inner))
    keep = 1.0 - rate
    weight = (rate * density) * (1.0 / 36.0)
    bx, by, bz = weight * vx, weight * vy, weight * vz
    half = 0.5 * weight
    ax, ay, az = half * vxx, half * vyy, half * vzz
    base = weight - (ax + ay + az) * (1.0 / 3.0)
    ex, ey, ez = base + ax, base + ay, base + az
    out = [None] * POPS
    out[0] = keep * f[0] + 12.0 * base
    for index, even, odd in ((1, ex, bx), (3, ey, by), (5, ez, bz)):
        out[index] = keep * f[index] + 2.0 * (even + odd)
        out[index + 1] = keep * f[index + 1] + 2.0 * (even - odd)
    for index, first, second, middle, mixed in (
        (7, bx, by, ex + ay, weight * vxy),
        (11, bx, bz, ex + az, weight * vxz),
        (15, by, bz, ey + az, weight * vyz),
    ):
        same, other = middle + mixed, middle - mixed
        plus, minus = first + second, first - second
        out[index] = keep * f[index] + (same + plus)
        out[index + 1] = keep * f[index + 1] + (same - plus)
        out[index + 2] = keep * f[index + 2] + (other + minus)
        out[index + 3] = keep * f[index + 3] + (other - minus)
    return out


def kernel(
    spans,
    streams,
    populations,
    camera_in,
    active_in,
    order_in,
    final,
    tile_image,
    camera,
    active_list,
    tile_order,
    field,
    post0,
    post1,
    post2,
    speed,
    strips,
    deep,
    second,
    rims,
    arrived,
    speed_rims,
    speed_arrived,
    shaded,
    foot,
    outgoing,
    incoming,
    send_sem,
    recv_sem,
    load_sem,
    own_sem,
    small_sem,
):
    stream = lax.axis_index("stream")
    span = lax.axis_index("span")
    stream_up = lax.rem(stream + 1, streams)
    stream_down = lax.rem(stream + streams - 1, streams)
    span_up = lax.rem(span + 1, spans)
    span_down = lax.rem(span + spans - 1, spans)
    span_far = lax.rem(span + 2, spans)

    barrier = pltpu.get_barrier_semaphore()
    partners = (
        (stream_up, span),
        (stream_down, span),
        (stream, span_up),
        (stream, span_down),
        (stream_up, span_up),
        (stream_up, span_down),
        (stream_down, span_up),
        (stream_down, span_down),
        (stream, span_far),
    )
    for partner in partners:
        pl.semaphore_signal(barrier, inc=1, device_id=partner, device_id_type=MESH)

    loads = [None] * COLUMNS
    for k in range(COLUMNS // 2):
        for column in (k, COLUMNS - 1 - k):
            loads[column] = pltpu.make_async_copy(
                populations.at[:, :, pl.ds(column * LANES, LANES)], field.at[:, column], load_sem.at[column]
            )
            loads[column].start()
    small = [
        pltpu.make_async_copy(source, target, small_sem.at[number])
        for number, (source, target) in enumerate(
            ((camera_in, camera), (active_in, active_list), (order_in, tile_order))
        )
    ]
    for copy in small:
        copy.start()

    lane = lax.broadcasted_iota(jnp.int32, (8, LANES), 1)
    upper = lane >= NZ
    level = lax.rem(lane, NZ)
    floor = level == 0
    ceiling = level == NZ - 1

    def remote(source, target, number, device):
        return pltpu.make_async_remote_copy(
            src_ref=source,
            dst_ref=target,
            send_sem=send_sem.at[number],
            recv_sem=recv_sem.at[number],
            device_id=device,
            device_id_type=MESH,
        )

    before_row, after_row = TOP - 1, TOP + PLANES
    before_place, after_place = 0, PLACES - 1

    def x_copies(buffer, up_strip, down_strip, up, down, depth, number):
        places = pl.ds(1, COLUMNS)
        return [
            remote(up_strip, buffer.at[pl.ds(*up), places, before_row - depth], number, (stream_up, span)),
            remote(down_strip, buffer.at[pl.ds(*down), places, after_row + depth], number + 1, (stream_down, span)),
        ]

    def y_copies(up_source, up_target, down_source, down_target, number):
        return [
            remote(up_source, up_target, number, (stream, span_up)),
            remote(down_source, down_target, number + 1, (stream, span_down)),
        ]

    corner_paths = (
        (7, 0, COLUMNS - 1, before_place, before_row, (stream_up, span_up)),
        (9, 0, 0, after_place, before_row, (stream_up, span_down)),
        (10, 1, COLUMNS - 1, before_place, after_row, (stream_down, span_up)),
        (8, 1, 0, after_place, after_row, (stream_down, span_down)),
    )

    def corner_copies(buffer, strip, number, first, count=1, depth=0):
        copies = []
        for index, side, column, place, row, device in corner_paths:
            slot = SLOT[index] if count == 1 else SLOT[3 if column else 4]
            outwards = -depth if row == before_row else depth
            copies.append(
                remote(
                    strip[side].at[pl.ds(slot - first[side], count), pl.ds(column, 1)],
                    buffer.at[pl.ds(slot, count), place, pl.ds(row + outwards, 1)],
                    number + len(copies),
                    device,
                )
            )
        return copies

    def joined(along_y, before, here, after):
        if along_y == 1:
            return jnp.where(upper, before(), here())
        if along_y == -1:
            return jnp.where(upper, here(), after())
        return here()

    def block_reader(buffer, place, block):
        def read(slot, along_y, plane):
            rows = pl.ds(TOP + 8 * block + plane, 8)
            return joined(
                along_y,
                lambda: buffer[slot, place - 1, rows],
                lambda: buffer[slot, place, rows],
                lambda: buffer[slot, place + 1, rows],
            )

        return read

    def strip_reader(buffer, plane, column):
        flat = buffer.reshape(buffer.shape[0], PLACES * ROWS, LANES)
        first = (column + 1) * ROWS + TOP + plane

        def read(slot, along_y, along):
            def at(step):
                return lambda: flat[slot, pl.ds(first + step * ROWS + along, 8, stride=ROWS)]

            return joined(along_y, at(-1), at(0), at(1))

        return read

    def rim_reader(buffer, block):
        def read(slot, along_y, plane):
            rows = pl.ds(TOP + 8 * block + plane, 8)
            high, low = {0: (COLUMNS, 1), 1: (0, COLUMNS), -1: (1, PLACES - 1)}[along_y]
            return jnp.where(upper, buffer[slot, high, rows], buffer[slot, low, rows])

        return read

    def streamed(read):
        values = []
        for index in range(POPS):
            along_x, along_y, along_z = VELOCITIES[index]
            value = read(SLOT[index], along_y, -along_x)
            shift = ((NZ if along_y else 0) + along_z) % LANES
            if shift:
                value = pltpu.roll(value, shift, 1)
            if along_z:
                value = jnp.where(
                    floor if along_z > 0 else ceiling, read(SLOT[OPPOSITE[index]], 0, 0), value
                )
            values.append(value)
        return values

    def sweep(work, first, last, step, blocks, start=0, stop=None):
        def body(k, carry):
            for part in range(step):
                work(first + step * k + part, blocks)
            return carry

        lax.fori_loop(start, (last - first) // step if stop is None else stop, body, 0)

    everything = tuple(range(BLOCKS))

    def inner(work, start=0, stop=None):
        sweep(work, 1, COLUMNS - 1, 7, (1, 2), start, stop)

    def outer(work):
        for column in (0, COLUMNS - 1):
            work(column, (1, 2))
        sweep(work, 0, COLUMNS, 8, (0, 3))

    sent = []

    def send(copies):
        for copy in copies:
            copy.start()
        sent.extend(copies)

    buffers = (post0, post1, post2)
    edge_strips = [(strips.at[phase, 0], strips.at[phase, 1]) for phase in range(2)]
    edge_strips.append((deep.at[0, pl.ds(*X_UP)], deep.at[1, pl.ds(*X_DOWN)]))
    x_sides, corners = [], []
    for phase, buffer in enumerate(buffers):
        number = phase * POST_MESSAGES
        x_sides.append(x_copies(buffer, *edge_strips[phase], X_UP, X_DOWN, 0, number))
        if phase < 2:
            corners.append(
                corner_copies(buffer, edge_strips[phase], number + 2, (X_UP[0], X_DOWN[0]))
            )
        else:
            corners.append(corner_copies(buffer, (deep.at[0], deep.at[1]), number + 2, (0, 0)))
    late = x_copies(
        post2, deep.at[0, pl.ds(*LATE_UP)], deep.at[1, pl.ds(*LATE_DOWN)], LATE_UP, LATE_DOWN, 0, LATE_BASE
    )
    late += x_copies(post2, second.at[0], second.at[1], X_UP, X_DOWN, 1, LATE_BASE + 2)
    late += corner_copies(post2, (deep.at[0], deep.at[1]), LATE_BASE + 4, (0, 0), count=3)
    late += corner_copies(
        post2, (second.at[0], second.at[1]), LATE_BASE + 8, (X_UP[0], X_DOWN[0]), depth=1
    )
    y_sides = [
        y_copies(
            rims.at[phase, 0],
            arrived.at[phase, 0],
            rims.at[phase, 1],
            arrived.at[phase, 1],
            phase * POST_MESSAGES + 6,
        )
        for phase in range(3)
    ]

    def post_strips(values_of, planes, store):
        for side in range(2):
            for half in range(2):
                out = collide(values_of(planes[side], 8 * half))
                store(side, pl.ds(8 * half, 8), out)

    def store_edges(phase):
        def store(side, rows, out):
            first, count = (X_UP, X_DOWN)[side]
            for place in range(count):
                strips[phase, side, place, rows] = out[ORDER[first + place]]

        return store

    def store_deep(side, rows, out):
        for index in range(POPS):
            deep[side, SLOT[index], rows] = out[index]

    def store_second(side, rows, out):
        first, count = (X_UP, X_DOWN)[side]
        for place in range(count):
            second[side, place, rows] = out[ORDER[first + place]]

    edge_planes, second_planes = (PLANES - 1, 0), (PLANES - 2, 1)

    def packed(side, own, other):
        turned = pltpu.roll(other, NZ, 1)
        return jnp.where(upper, turned, own) if side else jnp.where(upper, own, turned)

    def post_rims(phase, values_of):
        alone = []
        for block in range(BLOCKS):
            out = collide(values_of(block))
            for side in range(2):
                for pack, (first, second) in enumerate(Y_PACKS[side]):
                    rims[phase, side, pl.ds(pack * PLANES + 8 * block, 8)] = packed(side, out[first], out[second])
            alone.append([out[index] for index in Y_ALONE])
        for block in range(BLOCKS // 2):
            for side in range(2):
                rims[phase, side, pl.ds(2 * PLANES + 8 * block, 8)] = packed(
                    side, alone[block][side], alone[block + BLOCKS // 2][side]
                )

    def await_rims(phase):
        for copy in x_sides[phase] + corners[phase] + y_sides[phase]:
            copy.wait_recv()
        buffer = buffers[phase]
        for side, place in enumerate((before_place, after_place)):
            for block in range(BLOCKS):
                rows = pl.ds(TOP + 8 * block, 8)
                for pack, (first, second) in enumerate(Y_PACKS[side]):
                    value = arrived[phase, side, pl.ds(pack * PLANES + 8 * block, 8)]
                    buffer[SLOT[first], place, rows] = value
                    buffer[SLOT[second], place, rows] = pltpu.roll(value, NZ, 1)
            for block in range(BLOCKS // 2):
                value = arrived[phase, side, pl.ds(2 * PLANES + 8 * block, 8)]
                slot = SLOT[Y_ALONE[side]]
                buffer[slot, place, pl.ds(TOP + 8 * block, 8)] = value
                buffer[slot, place, pl.ds(TOP + PLANES // 2 + 8 * block, 8)] = pltpu.roll(value, NZ, 1)

    def post_column(target, column, blocks, values_of):
        for block in blocks:
            out = collide(values_of(block))
            for index in range(POPS):
                target[SLOT[index], column + 1, pl.ds(TOP + 8 * block, 8)] = out[index]

    def first_work(column, blocks):
        post_column(
            post0,
            column,
            blocks,
            lambda block: [field[index, column, pl.ds(8 * block, 8)] for index in range(POPS)],
        )

    for column in (0, COLUMNS - 1):
        loads[column].wait()
    post_rims(
        0,
        lambda block: [
            jnp.where(upper, field[index, COLUMNS - 1, pl.ds(8 * block, 8)], field[index, 0, pl.ds(8 * block, 8)])
            for index in range(POPS)
        ],
    )
    for column in range(1, COLUMNS - 1):
        loads[column].wait()
    flat_field = field.reshape(POPS, COLUMNS * PLANES, LANES)
    post_strips(
        lambda plane, column: [
            flat_field[index, pl.ds(column * PLANES + plane, 8, stride=PLANES)] for index in range(POPS)
        ],
        edge_planes,
        store_edges(0),
    )
    seam = (stream == 0).astype(jnp.int32)
    sweep(first_work, 0, COLUMNS, 4, everything, 0, 4 * seam)
    pl.semaphore_wait(barrier, len(partners))
    send(corners[0] + x_sides[0] + y_sides[0])
    sweep(first_work, 0, COLUMNS, 4, everything, 4 * seam)

    for phase in (1, 2):
        source, target = buffers[phase - 1], buffers[phase]

        def step_work(column, blocks):
            post_column(target, column, blocks, lambda block: streamed(block_reader(source, column + 1, block)))

        def strip_values(plane, column):
            return streamed(strip_reader(source, plane, column))

        inner(step_work)
        await_rims(phase - 1)
        post_strips(strip_values, edge_planes, store_edges(phase) if phase == 1 else store_deep)
        send(corners[phase] + x_sides[phase])
        if phase == 2:
            post_strips(strip_values, second_planes, store_second)
            send(late[4:] + late[:4])
        post_rims(phase, lambda block: streamed(rim_reader(source, block)))
        send(y_sides[phase])
        outer(step_work)

    def velocity(values):
        _, flow, _, _, density = moments(values)
        inverse = reciprocal(density)
        return [part * inverse for part in flow]

    def last_work(column, blocks):
        lanes = pl.ds(pl.multiple_of(column * LANES, LANES), LANES)
        for block in blocks:
            values = streamed(block_reader(post2, column + 1, block))
            for index in range(POPS):
                final[index, pl.ds(8 * block, 8), lanes] = values[index]
            for dimension, part in enumerate(velocity(values)):
                speed[dimension, column + 1, pl.ds(TOP + 8 * block, 8)] = part

    inner(last_work)
    await_rims(2)
    parts = [velocity(streamed(rim_reader(post2, block))) for block in range(BLOCKS)]
    for side in range(2):
        for block in range(BLOCKS):
            speed_rims[side, pl.ds(8 * block, 8)] = packed(side, parts[block][0], parts[block][1])
        for block in range(BLOCKS // 2):
            speed_rims[side, pl.ds(PLANES + 8 * block, 8)] = packed(
                side, parts[block][2], parts[block + BLOCKS // 2][2]
            )
    speed_y = y_copies(
        speed_rims.at[0], speed_arrived.at[0], speed_rims.at[1], speed_arrived.at[1], SPEED_BASE
    )
    send(speed_y)
    outer(last_work)

    for copy in small:
        copy.wait()

    bits = jnp.int32(0)
    for entry in range(32):
        number = active_list[entry]
        bits = bits | jnp.where(number < 32, jnp.left_shift(jnp.int32(1), jnp.minimum(number, 31)), 0)
    falling = jnp.full((8, LANES), camera[0], jnp.int32) == 1
    leading = falling == upper
    bits = jnp.full((8, LANES), bits, jnp.int32)
    corner = 4 * (lax.broadcasted_iota(jnp.int32, (8, LANES), 0) // 4)

    def shade_with(read, brick, store):
        centre = [read(dimension, 0, 0) for dimension in range(3)]
        slope_x, slope_y, slope_z = [], [], []
        for dimension in range(3):
            here = centre[dimension]
            slope_x.append(read(dimension, 0, 1) - read(dimension, 0, -1))
            slope_y.append(pltpu.roll(read(dimension, -1, 0) - read(dimension, 1, 0), NZ, 1))
            above = jnp.where(ceiling, -here, pltpu.roll(here, LANES - 1, 1))
            below = jnp.where(floor, -here, pltpu.roll(here, 1, 1))
            slope_z.append(above - below)
        cross = slope_x[1] * slope_y[0] + slope_x[2] * slope_z[0] + slope_y[2] * slope_z[1]
        total = slope_x[0] * slope_x[0] + slope_y[1] * slope_y[1] + slope_z[2] * slope_z[2] + (cross + cross)
        vortex = total * (-0.125 / VORTEX_SCALE)
        small = jnp.exp(-jnp.abs(vortex))
        one = 1.0 + small
        share = reciprocal(one)
        colours = [jnp.where(vortex >= 0.0, share, small * share)]
        for dimension in (0, 2):
            colours.append(reciprocal(1.0 + jnp.exp(centre[dimension] * (-1.0 / SPEED_SCALE))))
        passing = jnp.exp(-OPACITY_GAIN * (jnp.maximum(vortex, 0.0) + jnp.log(one)))
        passing = jnp.where((jnp.right_shift(bits, brick) & 1) == 1, passing, 1.0)
        other = pltpu.roll(passing, NZ, 1)
        weight = (1.0 - passing) * jnp.where(leading, 1.0, other)
        for number in range(3):
            store(number, colours[number] * weight)
        store(3, passing * other)

    def shade(column, blocks):
        for block in blocks:

            def store(number, value):
                shaded[number, column, pl.ds(8 * block, 8)] = value

            shade_with(block_reader(speed, column + 1, block), corner + (8 * block + column // 4), store)

    flat_shaded = shaded.reshape(4, COLUMNS * PLANES, LANES)

    def shade_strip(plane, first):
        def store(number, value):
            flat_shaded[number, pl.ds(first * PLANES + plane, 8, stride=PLANES)] = value

        brick = (lax.broadcasted_iota(jnp.int32, (8, LANES), 0) + first) // 4
        shade_with(strip_reader(speed, plane, first), brick + plane // 4 * 4, store)

    for plane in (-1, PLANES):
        for place in range(1, COLUMNS + 1):
            speed[:, place, pl.ds(TOP + plane, 1)] = jnp.zeros((3, 1, LANES), jnp.float32)
    sweep(shade, 1, COLUMNS - 1, 7, (1, 2))
    sweep(shade, 1, COLUMNS - 1, 7, (0, 3))
    for copy in late:
        copy.wait_recv()
    flat_speed = speed.reshape(3, PLACES * ROWS, LANES)
    for plane in (-1, PLANES):
        for first in (0, 8):
            for dimension, part in enumerate(velocity(streamed(strip_reader(post2, plane, first)))):
                flat_speed[dimension, pl.ds((first + 1) * ROWS + TOP + plane, 8, stride=ROWS)] = part
    for plane in (0, PLANES - 1):
        for first in (1, 7):
            shade_strip(plane, first)

    def walk(side, block, first, last, state):
        from_back = falling if side == 1 else jnp.logical_not(falling)
        colours, through = state[:3], state[3]
        for k in range(first, last, -1):
            column = k if side == 0 else COLUMNS - 1 - k
            pair = [shaded[number, column, pl.ds(8 * block, 8)] for number in range(4)]
            fade = jnp.where(from_back, pair[3], 1.0)
            veil = jnp.where(from_back, 1.0, through)
            colours = [colours[number] * fade + pair[number] * veil for number in range(3)]
            through = through * pair[3]
        return colours + [through]

    sums = {}
    for block in range(BLOCKS):
        for side in range(2):
            start = [jnp.zeros((8, LANES), jnp.float32)] * 3 + [jnp.ones((8, LANES), jnp.float32)]
            sums[side, block] = walk(side, block, COLUMNS // 2 - 1, 0, start)
    for copy in speed_y:
        copy.wait_recv()
    for side, place in enumerate((before_place, after_place)):
        for block in range(BLOCKS):
            value = speed_arrived[side, pl.ds(8 * block, 8)]
            rows = pl.ds(TOP + 8 * block, 8)
            speed[0, place, rows] = value
            speed[1, place, rows] = pltpu.roll(value, NZ, 1)
        for block in range(BLOCKS // 2):
            value = speed_arrived[side, pl.ds(PLANES + 8 * block, 8)]
            speed[2, place, pl.ds(TOP + 8 * block, 8)] = value
            speed[2, place, pl.ds(TOP + PLANES // 2 + 8 * block, 8)] = pltpu.roll(value, NZ, 1)
    for column in (0, COLUMNS - 1):
        shade(column, everything)
    for side, block in sums:
        sums[side, block] = walk(side, block, 0, -1, sums[side, block])

    for block in range(BLOCKS):
        low, high = sums[0, block], sums[1, block]
        front = [jnp.where(falling, b, a) for a, b in zip(low, high)]
        back = [jnp.where(falling, a, b) for a, b in zip(low, high)]
        for number in range(4):
            if number < 3:
                half = front[number] + front[3] * back[number]
                value = half + pltpu.roll(half, NZ, 1)
            else:
                value = front[3] * back[3]
            for part in range(2):
                foot[2 * block + part, pl.ds(4 * number, 4)] = value[4 * part : 4 * part + 4]

    for number in range(8):
        outgoing[number] = foot[tile_order[number]]
    tiles = []
    for hop, target in enumerate((span_far, span_up, span_down)):
        tiles.append(
            remote(
                outgoing.at[pl.ds(2 * target, 2)], incoming.at[span], TILE_BASE + hop, (stream, target)
            )
        )
    earlier = list(sent)
    send(tiles)
    own = pltpu.make_async_copy(outgoing.at[pl.ds(2 * span, 2)], incoming.at[span], own_sem)
    own.start()
    own.wait()
    for copy in earlier:
        copy.wait_send()
    for copy in tiles:
        copy.wait_recv()
    wide = jnp.broadcast_to(camera[0], (16, LANES)) == 1
    upper_row = lax.broadcasted_iota(jnp.int32, (1, LANES), 1) >= NZ
    for tile in range(2):
        sheets = [incoming[source, tile] for source in range(spans)]
        colour = sheets[0][:12]
        through = sheets[0][12:]
        for source in range(1, spans):
            sheet = sheets[source]
            fade = jnp.concatenate([sheet[12:]] * 3, axis=0)
            veil = jnp.concatenate([through] * 3, axis=0)
            colour = jnp.where(wide[:12], colour * fade + sheet[:12], colour + veil * sheet[:12])
            through = through * sheet[12:]
        for number in range(4):
            quad = colour[4 * number : 4 * number + 4] if number < 3 else through
            for part in range(2):
                tile_image[tile, pl.ds(number, 1), pl.ds(part * LANES, LANES)] = jnp.where(
                    upper_row, quad[2 * part + 1 : 2 * part + 2], quad[2 * part : 2 * part + 1]
                )

    for copy in tiles:
        copy.wait_send()


def store_kernel(final, tile_image, final_out, image_out, sems):
    copies = [
        pltpu.make_async_copy(final.at[index], final_out.at[index], sems.at[index]) for index in range(POPS)
    ]
    copies.append(pltpu.make_async_copy(tile_image, image_out, sems.at[POPS]))
    for copy in copies:
        copy.start()
    for copy in copies:
        copy.wait()


def on_device(populations, camera, active_list, tile_order):
    spans = lax.axis_size("span")
    streams = lax.axis_size("stream")
    vmem = functools.partial(pl.BlockSpec, memory_space=pltpu.VMEM)
    pinned = functools.partial(pltpu.with_memory_space_constraint, memory_space=pltpu.HBM)
    anywhere = functools.partial(pl.BlockSpec, memory_space=pl.ANY)
    post = pltpu.VMEM((POPS, PLACES, ROWS, LANES), jnp.float32)
    final, tile_image = pl.pallas_call(
        functools.partial(kernel, spans, streams),
        out_shape=(
            jax.ShapeDtypeStruct(populations.shape, jnp.float32),
            jax.ShapeDtypeStruct((2, 4, 256), jnp.float32),
        ),
        in_specs=[anywhere()] * 4,
        out_specs=(vmem(), vmem()),
        scratch_shapes=[
            pltpu.SMEM(camera.shape, jnp.int32),
            pltpu.SMEM((active_list.size,), jnp.int32),
            pltpu.SMEM((tile_order.size,), jnp.int32),
            pltpu.VMEM((POPS, COLUMNS, PLANES, LANES), jnp.float32),
            post,
            post,
            post,
            pltpu.VMEM((3, PLACES, ROWS, LANES), jnp.float32),
            pltpu.VMEM((2, 2, 5, COLUMNS, LANES), jnp.float32),
            pltpu.VMEM((2, POPS, COLUMNS, LANES), jnp.float32),
            pltpu.VMEM((2, 5, COLUMNS, LANES), jnp.float32),
            pltpu.VMEM((3, 2, RIM_ROWS, LANES), jnp.float32),
            pltpu.VMEM((3, 2, RIM_ROWS, LANES), jnp.float32),
            pltpu.VMEM((2, SPEED_ROWS, LANES), jnp.float32),
            pltpu.VMEM((2, SPEED_ROWS, LANES), jnp.float32),
            pltpu.VMEM((4, COLUMNS, PLANES, LANES), jnp.float32),
            pltpu.VMEM((8, 16, LANES), jnp.float32),
            pltpu.VMEM((8, 16, LANES), jnp.float32),
            pltpu.VMEM((spans, 2, 16, LANES), jnp.float32),
            pltpu.SemaphoreType.DMA((MESSAGES,)),
            pltpu.SemaphoreType.DMA((MESSAGES,)),
            pltpu.SemaphoreType.DMA((COLUMNS,)),
            pltpu.SemaphoreType.DMA,
            pltpu.SemaphoreType.DMA((3,)),
        ],
        compiler_params=pltpu.CompilerParams(
            collective_id=0, has_side_effects=True, vmem_limit_bytes=48 * 1024 * 1024
        ),
    )(populations, camera, pinned(active_list.reshape(-1)), pinned(tile_order.reshape(-1)))
    return pl.pallas_call(
        store_kernel,
        out_shape=(
            jax.ShapeDtypeStruct(final.shape, jnp.float32),
            jax.ShapeDtypeStruct(tile_image.shape, jnp.float32),
        ),
        in_specs=[anywhere()] * 2,
        out_specs=(anywhere(), anywhere()),
        scratch_shapes=[pltpu.SemaphoreType.DMA((POPS + 1,))],
        compiler_params=pltpu.CompilerParams(vmem_limit_bytes=1024 * 1024),
    )(final, tile_image)


def solution(mesh):
    placed = (P(None, "stream", "span"), P("stream"), P("stream", "span", None), P("stream", None))
    return jax.shard_map(
        on_device,
        mesh=mesh,
        in_specs=placed,
        out_specs=(P(None, "stream", "span"), P(("stream", "span"), None, None)),
        check_vma=False,
    )
```
